32 devices in a mesh: section: 4 (over y, core), dp: 8 (over z, x).
Axes of the slice: x: 2, y: 2, z: 4, core: 2. Of those that a mesh axis runs over, the one named last changes fastest.
Arguments:
- crop_maps: bfloat16 [8, 4, 2, 8, 8, 640], P('dp'), may hold values from -6 to 6
- target_maps: int32 [8, 4, 2, 8, 8], P('dp'), may hold values 0 or 1
- crop_counts: int32 [8, 4], P('dp'), may hold values from 1 to 2, as said below
- depth_kernels: float32 [4, 49, 640], P('section'), may hold values from -0.875 to 0.875
- weight_in: bfloat16 [4, 640, 2560], P('section', 'dp'), may hold values from -0.25 to 0.25
- weight_out: bfloat16 [4, 2560, 640], P('section', 'dp'), may hold values from -0.125 to 0.125
- head_weight: float32 [640], replicated, may hold values from -0.25 to 0.25
Outputs:
- grad_in: float32 [4, 640, 2560], P('section', 'dp')
- grad_out: float32 [4, 2560, 640], P('section', 'dp')
- grad_kernels: float32 [4, 49, 640], P('section')
- grad_head: float32 [640], replicated
- loss_value: float32 [], replicated
The draws below stay inside these ranges and needn't reach their ends.
Inputs may be any that keep to these rules, and one draw needn't show every extreme that they name: `crop_counts`: every data group has some micro-batch with exactly 2 crops.
All inputs are finite; a program needn't handle non-finite values. No bound on the sum of `target_maps` on one device may be relied on, other than what follows from the above.
Results may differ from the reference program's by a relative error of at most 0.034.
Values may be sent and summed in bfloat16 or wider, within the bound.
A program may use at most 128 MiB of HBM per device.

```python
import jax
import jax.numpy as jnp
from jax import lax

C = 640
H = 2560
P_SIZE = 8
M = 4
CAP = 2
SECTIONS = 4
GROUPS = 8


def draw_crop_counts(key, part):
    base = jax.random.randint(jax.random.fold_in(key, 11), (GROUPS, M), 1, CAP + 1, dtype=jnp.int32)
    chosen = jax.random.randint(jax.random.fold_in(key, 12), (GROUPS, 1), 0, M, dtype=jnp.int32)
    return jnp.where(jnp.arange(M, dtype=jnp.int32)[None, :] == chosen, CAP, base).astype(jnp.int32)


def touch_ends(array, own_key, smallest, largest):
    longest = array.shape.index(max(array.shape))
    spots = []
    for shift in (0, 1):
        where = [jax.random.randint(jax.random.fold_in(own_key, axis), (), 0, length) for axis, length in enumerate(array.shape)]
        where[longest] = (where[longest] + shift) % array.shape[longest]
        spots.append(tuple(where))
    return array.at[spots[0]].set(smallest).at[spots[1]].set(largest)


def block_scale(rng, shape, split, low, largest):
    def one(position, shards_of):
        draws = jax.random.uniform(jax.random.fold_in(jax.random.fold_in(rng, 6), position), (shards_of,), jnp.float32, low / len(split), largest / len(split))
        return jnp.repeat(jnp.exp(draws), shape[position] // shards_of).reshape((-1,) + (1,) * (len(shape) - position - 1))

    level = one(*split[0])
    for cut in split[1:]:
        level = level * one(*cut)
    return level


def scatter_about(key, dims, scale, most, shards=(), kind=jnp.bfloat16):
    values = jax.random.normal(key, dims, jnp.float32) * scale
    if len(shards) > 0:
        values = block_scale(key, dims, shards, -0.22, 0.18) * values
    return jnp.clip(values, min=-most, max=most).astype(kind)


def setup_inputs(seed: int = 0) -> dict:
    key_of = jax.random.split(jax.random.key(seed), 8)
    crop_maps = scatter_about(key_of[0], (GROUPS, M, CAP, P_SIZE, P_SIZE, C), 1.0, 6.0, ((0, 8),))
    target_maps = touch_ends((jax.random.randint(key_of[1], (GROUPS, M, CAP, P_SIZE, P_SIZE), 0, 5) < 2).astype(jnp.int32), jax.random.fold_in(key_of[1], 1), 0, 1)
    crop_counts = draw_crop_counts(jax.random.fold_in(key_of[7], 71), 0)
    depth_kernels = scatter_about(key_of[3], (SECTIONS, 49, C), 49 ** -0.5, 0.875, ((0, 4),), jnp.float32)
    weight_in = scatter_about(key_of[4], (SECTIONS, C, H), C ** -0.5, 0.25, ((0, 4), (1, 8)))
    weight_out = scatter_about(key_of[5], (SECTIONS, H, C), H ** -0.5, 0.125, ((0, 4), (1, 8)))
    head_weight = scatter_about(key_of[6], (C,), C ** -0.5, 0.25, (), jnp.float32)
    return dict(crop_maps=crop_maps, target_maps=target_maps, crop_counts=crop_counts, depth_kernels=depth_kernels, weight_in=weight_in, weight_out=weight_out, head_weight=head_weight)


EPSILON = 1e-06
SQRT_HALF = 0.7071067811865476
INV_ROOT_TWO_PI = 0.3989422804014327

def depthwise(values, kernel):
    side = values.shape[1]
    padded = jnp.pad(values, ((0, 0), (3, 3), (3, 3), (0, 0)))
    result = jnp.zeros_like(values)
    for vertical in range(7):
        for across in range(7):
            result = result + padded[:, vertical:vertical + side, across:across + side, :] * kernel[vertical * 7 + across]
    return result

def depthwise_back(grads, kernel):
    side = grads.shape[1]
    padded = jnp.pad(grads, ((0, 0), (3, 3), (3, 3), (0, 0)))
    result = jnp.zeros_like(grads)
    for vertical in range(7):
        for across in range(7):
            result = result + padded[:, 6 - vertical:6 - vertical + side, 6 - across:6 - across + side, :] * kernel[vertical * 7 + across]
    return result

def kernel_grad(values, grads):
    side = values.shape[1]
    padded = jnp.pad(values, ((0, 0), (3, 3), (3, 3), (0, 0)))
    taps = []
    for vertical in range(7):
        for across in range(7):
            taps.append(lax.optimization_barrier(jnp.sum(padded[:, vertical:vertical + side, across:across + side, :] * grads, axis=(0, 1, 2))))
    return jnp.stack(taps, axis=0)

def block_parts(tiles, kernel, weight_in):
    width = tiles.shape[-1]
    widened = tiles.astype(jnp.float32)
    mixed = depthwise(widened, kernel).reshape(-1, width)
    centred = mixed - lax.optimization_barrier(jnp.mean(mixed, axis=-1, keepdims=True))
    inverse = lax.rsqrt(lax.optimization_barrier(jnp.mean(centred * centred, axis=-1, keepdims=True)) + EPSILON)
    normed = centred * inverse
    normed_low = normed.astype(jnp.bfloat16)
    hidden = jnp.dot(normed_low, weight_in, preferred_element_type=jnp.float32)
    activated = (hidden * 0.5 * (1.0 + lax.erf(hidden * SQRT_HALF))).astype(jnp.bfloat16)
    return (widened, normed, inverse, normed_low, hidden, activated)

def block_forward(tiles, kernel, weight_in, weight_out):
    width = tiles.shape[-1]
    widened, normed, inverse, normed_low, hidden, activated = block_parts(tiles, kernel, weight_in)
    output = jnp.dot(activated, weight_out, preferred_element_type=jnp.float32)
    return (widened.reshape(-1, width) + output).astype(jnp.bfloat16).reshape(tiles.shape)

def block_backward(tiles, upstream, kernel, weight_in, weight_out):
    width = tiles.shape[-1]
    widened, normed, inverse, normed_low, hidden, activated = block_parts(tiles, kernel, weight_in)
    up_flat = upstream.reshape(-1, width)
    through = lax.dot_general(up_flat, weight_out, (((1,), (1,)), ((), ())), preferred_element_type=jnp.float32)
    slope = 0.5 * (1.0 + lax.erf(hidden * SQRT_HALF)) + hidden * jnp.exp(-0.5 * hidden * hidden) * INV_ROOT_TWO_PI
    hidden_grad = (through * slope).astype(jnp.bfloat16)
    normed_grad = lax.dot_general(hidden_grad, weight_in, (((1,), (1,)), ((), ())), preferred_element_type=jnp.float32)
    mixed_grad = inverse * (normed_grad - lax.optimization_barrier(jnp.mean(normed_grad, axis=-1, keepdims=True)) - normed * lax.optimization_barrier(jnp.mean(normed_grad * normed, axis=-1, keepdims=True)))
    mixed_tiles = mixed_grad.reshape(tiles.shape)
    kernel_term = kernel_grad(widened, mixed_tiles)
    tile_grad = (upstream.astype(jnp.float32) + depthwise_back(mixed_tiles, kernel)).astype(jnp.bfloat16)
    return (tile_grad, kernel_term, normed_low, hidden_grad, activated, up_flat)

def outer_sum(left, right):
    return lax.dot_general(left, right, (((0,), (0,)), ((), ())), preferred_element_type=jnp.float32)

def head_terms(final, targets, live, head_weight, factor):
    widened = final.astype(jnp.float32)
    logits = lax.optimization_barrier(jnp.sum(widened * head_weight, axis=-1))
    weight_live = live.astype(jnp.float32)[:, :, None, None]
    truth = targets.astype(jnp.float32)
    loss_term = jnp.sum(weight_live * (jax.nn.softplus(logits) - truth * logits)) * factor
    logit_grad = (jax.nn.sigmoid(logits) - truth) * weight_live * factor
    seeds = (logit_grad[..., None] * head_weight).astype(jnp.bfloat16)
    head_term = lax.optimization_barrier(jnp.sum(logit_grad[..., None] * widened, axis=(0, 1, 2, 3)))
    return (loss_term, seeds, head_term)

def reference(crop_maps, target_maps, crop_counts, depth_kernels, weight_in, weight_out, head_weight):
    factor = 1.0 / (M * CAP)

    def per_group(carry, group):
        acc_in, acc_out, acc_kernel, acc_head, acc_loss = carry
        crops, targets, counts = group
        live = jnp.arange(CAP)[None, :] < counts[:, None]
        current = (crops * live[:, :, None, None, None].astype(jnp.bfloat16)).reshape(M * CAP, P_SIZE, P_SIZE, C)
        saved = []
        for layer in range(SECTIONS):
            saved.append(current)
            current = block_forward(current, depth_kernels[layer], weight_in[layer], weight_out[layer])
        loss_term, seeds, head_term = head_terms(current.reshape(M, CAP, P_SIZE, P_SIZE, C), targets, live, head_weight, factor)
        upstream = seeds.reshape(M * CAP, P_SIZE, P_SIZE, C)
        for layer in range(SECTIONS - 1, -1, -1):
            upstream, kernel_term, normed_low, hidden_grad, activated, up_flat = block_backward(saved[layer], upstream, depth_kernels[layer], weight_in[layer], weight_out[layer])
            acc_in = acc_in.at[layer].add(outer_sum(normed_low, hidden_grad))
            acc_out = acc_out.at[layer].add(outer_sum(activated, up_flat))
            acc_kernel = acc_kernel.at[layer].add(kernel_term)
        return ((acc_in, acc_out, acc_kernel, acc_head + head_term, acc_loss + loss_term), None)
    start = (jnp.zeros((SECTIONS, C, H), jnp.float32), jnp.zeros((SECTIONS, H, C), jnp.float32), jnp.zeros((SECTIONS, 49, C), jnp.float32), jnp.zeros((C,), jnp.float32), jnp.zeros((), jnp.float32))
    result, _ = lax.scan(per_group, start, (crop_maps, target_maps, crop_counts))
    return (result[0], result[1], result[2], result[3], result[4])
```

```python
import functools

import jax
import jax.numpy as jnp
from jax import lax
from jax.experimental import pallas as pl
from jax.experimental.pallas import tpu as pltpu
from jax.sharding import PartitionSpec as P

EPSILON = 1e-06
SQRT_HALF = 0.7071067811865476
INV_ROOT_TWO_PI = 0.3989422804014327
MESH = pl.DeviceIdType.MESH
LANES = 128
CHUNK = 512
TAPS = 7
SIDE = 8
SMALL_ROWS = 64
HEAD_ROW = 56


def shift_columns(values, distance):
    if distance == 0:
        return values
    column = lax.broadcasted_iota(jnp.int32, values.shape, 2)
    moved = pltpu.roll(values, (-distance) % SIDE, 2)
    keep = (column + distance >= 0) & (column + distance < SIDE)
    return jnp.where(keep, moved, 0.0)


def valid_rows(offset):
    return range(max(0, -offset), min(SIDE, SIDE - offset))


def depthwise(values, taps_ref, lanes, flip):
    rows = [jnp.zeros_like(values[:, 0]) for _ in range(SIDE)]
    for across in range(TAPS):
        shifted = shift_columns(values, across - 3)
        for vertical in range(TAPS):
            tap = vertical * TAPS + across
            if flip:
                tap = TAPS * TAPS - 1 - tap
            weight = taps_ref[pl.ds(tap, 1), lanes].reshape(1, 1, LANES)
            for row in valid_rows(vertical - 3):
                rows[row] = rows[row] + shifted[:, row + vertical - 3] * weight
    return jnp.stack(rows, axis=1)


def lane_tile(index):
    return pl.ds(pl.multiple_of(index * LANES, LANES), LANES)


def kernel(
    section_count, micro_count, slots,
    x_ref, target_ref, live_ref, taps_ref, first_ref, second_ref, head_ref,
    grad_in_ref, grad_out_ref, small_ref,
    tiles, results, ups, tile_grads, mixed, normed, normed_low, inverse, activated, slope,
    hidden_grad, kernel_acc, head_block,
    tile_send, tile_recv, up_send, up_recv, head_send, head_recv,
):
    section = lax.axis_index("section")
    last = section_count - 1
    cells = slots * SIDE * SIDE
    width = x_ref.shape[-1]
    expand = first_ref.shape[1]
    lane_tiles = width // LANES
    is_first = section == 0
    is_last = section == last
    following = jnp.minimum(section + 1, last)
    previous = jnp.maximum(section - 1, 0)

    barrier = pltpu.get_barrier_semaphore()
    for step in range(1, section_count):
        peer = lax.rem(section + step, section_count)
        pl.semaphore_signal(barrier, inc=1, device_id={"section": peer}, device_id_type=MESH)
    pl.semaphore_wait(barrier, section_count - 1)

    def rows_of(micro):
        return pl.ds(pl.multiple_of(micro * cells, cells), cells)

    def tile_copy(micro):
        return pltpu.make_async_remote_copy(
            src_ref=results.at[micro], dst_ref=tiles.at[micro],
            send_sem=tile_send.at[micro], recv_sem=tile_recv.at[micro],
            device_id={"section": following}, device_id_type=MESH,
        )

    def up_copy(micro):
        return pltpu.make_async_remote_copy(
            src_ref=tile_grads.at[micro], dst_ref=ups.at[micro],
            send_sem=up_send.at[micro], recv_sem=up_recv.at[micro],
            device_id={"section": previous}, device_id_type=MESH,
        )

    def head_copy(step):
        peer = lax.rem(section + step, section_count)
        return pltpu.make_async_remote_copy(
            src_ref=head_block, dst_ref=head_block,
            send_sem=head_send.at[step - 1], recv_sem=head_recv,
            device_id={"section": peer}, device_id_type=MESH,
        )

    @pl.when(is_last)
    def _():
        head_block[...] = jnp.zeros_like(head_block)

    def forward(micro, carry):
        @pl.when(is_first)
        def _():
            tiles[micro] = x_ref[micro]

        @pl.when(jnp.logical_not(is_first))
        def _():
            tile_copy(micro).wait_recv()

        def mix(index, carry):
            lanes = lane_tile(index)
            values = tiles[micro, :, lanes].astype(jnp.float32)
            values = values.reshape(slots, SIDE, SIDE, LANES)
            mixed[:, lanes] = depthwise(values, taps_ref, lanes, False).reshape(cells, LANES)
            return carry

        lax.fori_loop(0, lane_tiles, mix, 0)
        rows = rows_of(micro)
        value = mixed[...]
        centred = value - jnp.mean(value, axis=-1, keepdims=True)
        scale = lax.rsqrt(jnp.mean(centred * centred, axis=-1, keepdims=True) + EPSILON)
        unit = centred * scale
        low = unit.astype(jnp.bfloat16)
        normed[rows, :] = unit
        normed_low[rows, :] = low
        inverse[rows, :] = jnp.broadcast_to(scale, (cells, LANES))
        total = tiles[micro].astype(jnp.float32)
        for start in range(0, expand, CHUNK):
            columns = slice(start, start + CHUNK)
            hidden = jnp.dot(low, first_ref[:, columns], preferred_element_type=jnp.float32)
            portion = 0.5 * (1.0 + lax.erf(hidden * SQRT_HALF))
            active = (hidden * portion).astype(jnp.bfloat16)
            activated[rows, columns] = active
            slope[rows, columns] = (
                portion + hidden * jnp.exp(-0.5 * hidden * hidden) * INV_ROOT_TWO_PI
            )
            total = total + jnp.dot(
                active, second_ref[columns, :], preferred_element_type=jnp.float32
            )
        results[micro] = total.astype(jnp.bfloat16)

        @pl.when(jnp.logical_not(is_last))
        def _():
            tile_copy(micro).start()

        @pl.when(is_last)
        def _():
            final = results[micro].astype(jnp.float32)
            logits = jnp.sum(final * head_ref[...], axis=-1, keepdims=True)
            weight = live_ref[micro]
            truth = target_ref[micro]
            factor = 1.0 / (micro_count * slots)
            softplus = jnp.maximum(logits, 0.0) + jnp.log1p(jnp.exp(-jnp.abs(logits)))
            loss = jnp.sum(weight * (softplus - truth * logits)) * factor
            logit_grad = (1.0 / (1.0 + jnp.exp(-logits)) - truth) * weight * factor
            ups[micro] = (logit_grad * head_ref[...]).astype(jnp.bfloat16)
            term = jnp.sum(logit_grad * final, axis=0, keepdims=True)
            head_block[0:1, :] += term
            head_block[1:2, :] += jnp.full((1, width), loss)

        return carry

    lax.fori_loop(0, micro_count, forward, 0)

    @pl.when(is_last)
    def _():
        for step in range(1, section_count):
            head_copy(step).start()

    def backward(micro, carry):
        @pl.when(jnp.logical_not(is_last))
        def _():
            up_copy(micro).wait_recv()

        rows = rows_of(micro)
        upstream = ups[micro]
        total = jnp.zeros((cells, width), jnp.float32)
        for start in range(0, expand, CHUNK):
            columns = slice(start, start + CHUNK)
            through = lax.dot_general(
                upstream, second_ref[columns, :], (((1,), (1,)), ((), ())),
                preferred_element_type=jnp.float32,
            )
            grad = (through * slope[rows, columns]).astype(jnp.bfloat16)
            hidden_grad[rows, columns] = grad
            total = total + lax.dot_general(
                grad, first_ref[:, columns], (((1,), (1,)), ((), ())),
                preferred_element_type=jnp.float32,
            )
        unit = normed[rows, :]
        mixed_grad = inverse[rows, 0:1] * (
            total
            - jnp.mean(total, axis=-1, keepdims=True)
            - unit * jnp.mean(total * unit, axis=-1, keepdims=True)
        )
        normed[rows, :] = mixed_grad

        def unmix(index, carry):
            lanes = lane_tile(index)
            values = normed[rows, lanes].reshape(slots, SIDE, SIDE, LANES)
            back = depthwise(values, taps_ref, lanes, True).reshape(cells, LANES)
            back = back + ups[micro, :, lanes].astype(jnp.float32)
            tile_grads[micro, :, lanes] = back.astype(jnp.bfloat16)
            return carry

        @pl.when(jnp.logical_not(is_first))
        def _():
            lax.fori_loop(0, lane_tiles, unmix, 0)
            up_copy(micro).start()

        return carry

    lax.fori_loop(0, micro_count, backward, 0)

    upstreams = ups[...].reshape(micro_count * cells, width)
    for start in range(0, expand, CHUNK):
        columns = slice(start, start + CHUNK)
        grad_out_ref[columns, :] = lax.dot_general(
            activated[:, columns], upstreams, (((0,), (0,)), ((), ())),
            preferred_element_type=jnp.float32,
        ).astype(jnp.bfloat16)
    for start in range(0, expand, CHUNK):
        columns = slice(start, start + CHUNK)
        grad_in_ref[:, columns] = lax.dot_general(
            normed_low[...], hidden_grad[:, columns], (((0,), (0,)), ((), ())),
            preferred_element_type=jnp.float32,
        ).astype(jnp.bfloat16)

    kernel_acc[...] = jnp.zeros_like(kernel_acc)

    def tap_grads(flat, carry):
        micro = flat // lane_tiles
        lanes = lane_tile(flat % lane_tiles)
        values = tiles[micro, :, lanes].astype(jnp.float32)
        values = values.reshape(slots, SIDE, SIDE, LANES)
        grads = normed[rows_of(micro), lanes].reshape(slots, SIDE, SIDE, LANES)
        for across in range(TAPS):
            shifted = shift_columns(values, across - 3)
            for vertical in range(TAPS):
                offset = vertical - 3
                low, high = max(0, -offset), min(SIDE, SIDE - offset)
                product = shifted[:, low + offset : high + offset] * grads[:, low:high]
                kernel_acc[vertical * TAPS + across, :, lanes] += jnp.sum(product, axis=(0, 1))
        return carry

    lax.fori_loop(0, micro_count * lane_tiles, tap_grads, 0)
    small_ref[0:HEAD_ROW, :] = jnp.sum(kernel_acc[...], axis=1)

    @pl.when(is_last)
    def _():
        for step in range(1, section_count):
            head_copy(step).wait_send()

    @pl.when(jnp.logical_not(is_last))
    def _():
        head_copy(1).wait_recv()

    small_ref[HEAD_ROW:SMALL_ROWS, :] = head_block[...]

    def finish(micro, carry):
        @pl.when(jnp.logical_not(is_last))
        def _():
            tile_copy(micro).wait_send()

        @pl.when(jnp.logical_not(is_first))
        def _():
            up_copy(micro).wait_send()

        return carry

    lax.fori_loop(0, micro_count, finish, 0)


def body(crop_maps, target_maps, crop_counts, depth_kernels, weight_in, weight_out, head_weight):
    section_count = lax.axis_size("section")
    micro_count, slots = crop_maps.shape[1:3]
    width = crop_maps.shape[-1]
    cells = slots * SIDE * SIDE
    expand = weight_in.shape[2]
    live = jnp.arange(slots)[None, :] < crop_counts[0][:, None]
    entering = crop_maps[0] * live[:, :, None, None, None].astype(jnp.bfloat16)
    entering = entering.reshape(micro_count, cells, width)
    targets = target_maps[0].reshape(micro_count, cells, 1).astype(jnp.float32)
    weights = jnp.broadcast_to(
        live[:, :, None].astype(jnp.float32), (micro_count, slots, SIDE * SIDE)
    ).reshape(micro_count, cells, 1)
    first_full = lax.all_gather(weight_in[0], "dp", axis=0, tiled=True)
    second_full = lax.all_gather(weight_out[0], "dp", axis=0, tiled=True)
    low, full = jnp.bfloat16, jnp.float32
    every = micro_count * cells
    in_vmem = pl.BlockSpec(memory_space=pltpu.VMEM)
    grad_in, grad_out, small = pl.pallas_call(
        functools.partial(kernel, section_count, micro_count, slots),
        out_shape=(
            jax.ShapeDtypeStruct((width, expand), low),
            jax.ShapeDtypeStruct((expand, width), low),
            jax.ShapeDtypeStruct((SMALL_ROWS, width), full),
        ),
        in_specs=[in_vmem] * 7,
        out_specs=(in_vmem,) * 3,
        scratch_shapes=[
            pltpu.VMEM((micro_count, cells, width), low),
            pltpu.VMEM((micro_count, cells, width), low),
            pltpu.VMEM((micro_count, cells, width), low),
            pltpu.VMEM((micro_count, cells, width), low),
            pltpu.VMEM((cells, width), full),
            pltpu.VMEM((every, width), full),
            pltpu.VMEM((every, width), low),
            pltpu.VMEM((every, LANES), full),
            pltpu.VMEM((every, expand), low),
            pltpu.VMEM((every, expand), full),
            pltpu.VMEM((every, expand), low),
            pltpu.VMEM((HEAD_ROW, SIDE, width), full),
            pltpu.VMEM((SMALL_ROWS - HEAD_ROW, width), full),
            pltpu.SemaphoreType.DMA((micro_count,)),
            pltpu.SemaphoreType.DMA((micro_count,)),
            pltpu.SemaphoreType.DMA((micro_count,)),
            pltpu.SemaphoreType.DMA((micro_count,)),
            pltpu.SemaphoreType.DMA((section_count - 1,)),
            pltpu.SemaphoreType.DMA,
        ],
        compiler_params=pltpu.CompilerParams(
            collective_id=0, has_side_effects=True, vmem_limit_bytes=56 * 1024 * 1024
        ),
        cost_estimate=pl.CostEstimate(
            flops=12 * every * width * expand, bytes_accessed=8 * width * expand, transcendentals=0
        ),
    )(entering, targets, weights, depth_kernels[0], first_full, second_full, head_weight[None])
    grad_in_part = lax.psum_scatter(grad_in, "dp", scatter_dimension=0, tiled=True)
    grad_out_part = lax.psum_scatter(grad_out, "dp", scatter_dimension=0, tiled=True)
    small_total = lax.psum(small, "dp")
    taps = depth_kernels.shape[1]
    return (
        grad_in_part.astype(full)[None],
        grad_out_part.astype(full)[None],
        small_total[:taps][None],
        small_total[HEAD_ROW],
        small_total[HEAD_ROW + 1, 0],
    )


def solution(mesh):
    return jax.shard_map(
        body,
        mesh=mesh,
        in_specs=(
            P("dp", None, None, None, None, None),
            P("dp", None, None, None, None),
            P("dp", None),
            P("section", None, None),
            P("section", "dp", None),
            P("section", "dp", None),
            P(),
        ),
        out_specs=(
            P("section", "dp", None),
            P("section", "dp", None),
            P("section", None, None),
            P(),
            P(),
        ),
        check_vma=False,
    )
```

```python
import functools

import jax
import jax.numpy as jnp
from jax import lax
from jax.experimental import pallas as pl
from jax.experimental.pallas import tpu as pltpu
from jax.sharding import PartitionSpec as P

EPSILON = 1e-06
SQRT_HALF = 0.7071067811865476
INV_ROOT_TWO_PI = 0.3989422804014327
MESH = pl.DeviceIdType.MESH
LANES = 128
CHUNK = 512
TAPS = 7
SIDE = 8
SMALL_ROWS = 64
HEAD_ROW = 56


def shift_columns(values, distance):
    if distance == 0:
        return values
    column = lax.broadcasted_iota(jnp.int32, values.shape, 2)
    moved = pltpu.roll(values, (-distance) % SIDE, 2)
    keep = (column + distance >= 0) & (column + distance < SIDE)
    return jnp.where(keep, moved, 0.0)


def valid_rows(offset):
    return range(max(0, -offset), min(SIDE, SIDE - offset))


def depthwise(values, taps_ref, lanes, flip):
    rows = [jnp.zeros_like(values[:, 0]) for _ in range(SIDE)]
    for across in range(TAPS):
        shifted = shift_columns(values, across - 3)
        for vertical in range(TAPS):
            tap = vertical * TAPS + across
            if flip:
                tap = TAPS * TAPS - 1 - tap
            weight = taps_ref[pl.ds(tap, 1), lanes].reshape(1, 1, LANES)
            for row in valid_rows(vertical - 3):
                rows[row] = rows[row] + shifted[:, row + vertical - 3] * weight
    return jnp.stack(rows, axis=1)


def lane_tile(index):
    return pl.ds(pl.multiple_of(index * LANES, LANES), LANES)


class Links:
    def __init__(self, group, group_count, across_count):
        self.group = group
        self.across_count = across_count
        self.along_count = group_count // across_count
        self.along = group // across_count
        self.across = lax.rem(group, across_count)

    def at(self, along, across):
        return along * self.across_count + across

    def beside(self, step):
        return lax.rem(self.across + step, self.across_count)

    def far_first(self, turn):
        low_half = self.along < self.along_count // 2
        return jnp.where(low_half, self.along_count - 1 - turn, turn)

    def next(self, way):
        if way == 0:
            there = self.along + 1 < self.along_count
            place = jnp.minimum(self.along + 1, self.along_count - 1)
        else:
            there = self.along > 0
            place = jnp.maximum(self.along - 1, 0)
        return there, self.at(place, self.across)


def slab(ref, place, height):
    return ref.at[pl.ds(pl.multiple_of(place * height, 16), height), :]


def gather_copies(links, weights, recv, line, side):
    def copy(which, along, source, send_sem, peer):
        own, full = weights[which]
        origin = links.at(along, links.across)
        target = slab(full, origin, own.shape[0])
        return pltpu.make_async_remote_copy(
            src_ref=own if source else target, dst_ref=target,
            send_sem=send_sem, recv_sem=recv.at[which, origin],
            device_id={"dp": peer}, device_id_type=MESH,
        )

    def to_line(which, along, way, source=False):
        return copy(which, along, source, line.at[which, way, along], links.next(way)[1])

    def to_side(which, along, step, source=False):
        peer = links.at(links.along, links.beside(step))
        return copy(which, along, source, side.at[which, step - 1, along], peer)

    def arrival(which, along, across):
        own, full = weights[which]
        origin = links.at(along, across)
        target = slab(full, origin, own.shape[0])
        return pltpu.make_async_remote_copy(
            src_ref=own, dst_ref=target, send_sem=line.at[which, 0, 0],
            recv_sem=recv.at[which, origin],
            device_id={"dp": links.next(0)[1]}, device_id_type=MESH,
        )

    return to_line, to_side, arrival


def origin_at(links, distance, way):
    if way == 0:
        return links.along >= distance, jnp.maximum(links.along - distance, 0)
    last = links.along_count - 1
    return links.along + distance <= last, jnp.minimum(links.along + distance, last)


def gather(links, weights, recv, line, side):
    to_line, to_side, arrival = gather_copies(links, weights, recv, line, side)
    for which in range(2):
        for way in range(2):
            @pl.when(links.next(way)[0])
            def _():
                to_line(which, links.along, way, True).start()

        for step in range(1, links.across_count):
            to_side(which, links.along, step, True).start()
    for which in range(2):
        own, full = weights[which]
        height = own.shape[0]
        full[pl.ds(pl.multiple_of(links.group * height, 16), height), :] = own[...]
    for distance in range(1, links.along_count):
        for which in range(2):
            for way in range(2):
                present, along = origin_at(links, distance, way)

                @pl.when(present)
                def _():
                    arrival(which, along, links.across).wait_recv()

                    @pl.when(links.next(way)[0])
                    def _():
                        to_line(which, along, way).start()

                    for step in range(1, links.across_count):
                        to_side(which, along, step).start()

    for which in range(2):
        for along in range(links.along_count):
            for step in range(1, links.across_count):
                arrival(which, along, links.beside(step)).wait_recv()


def wait_gather_sends(links, weights, recv, line, side):
    to_line, to_side, _ = gather_copies(links, weights, recv, line, side)
    for which in range(2):
        for distance in range(links.along_count):
            for way in range(2):
                present, along = origin_at(links, distance, way)

                @pl.when(present & links.next(way)[0])
                def _():
                    to_line(which, along, way).wait_send()

        for along in range(links.along_count):
            for step in range(1, links.across_count):
                to_side(which, along, step).wait_send()


class Scatter:
    def __init__(self, links, sums, sides, lines, side_send, side_recv, line_send, line_recv):
        self.links, self.sums, self.sides, self.lines = links, sums, sides, lines
        self.side_send, self.side_recv = side_send, side_recv
        self.line_send, self.line_recv = line_send, line_recv

    def side_copy(self, which, step, along):
        links, buffer = self.links, self.sides[which]
        peer = links.at(links.along, links.beside(step))
        source = slab(self.sums[which], links.at(along, links.beside(step)), buffer.shape[2])
        return pltpu.make_async_remote_copy(
            src_ref=source, dst_ref=buffer.at[step - 1, along],
            send_sem=self.side_send.at[which, step - 1, along],
            recv_sem=self.side_recv.at[which, step - 1, along],
            device_id={"dp": peer}, device_id_type=MESH,
        )

    def line_copy(self, which, way, along):
        links, buffer = self.links, self.lines[which]
        source = slab(self.sums[which], links.at(along, links.across), buffer.shape[2])
        return pltpu.make_async_remote_copy(
            src_ref=source, dst_ref=buffer.at[way, along],
            send_sem=self.line_send.at[which, way, along],
            recv_sem=self.line_recv.at[which, way, along],
            device_id={"dp": links.next(way)[1]}, device_id_type=MESH,
        )

    def start_side(self, which, along):
        for step in range(1, self.links.across_count):
            self.side_copy(which, step, along).start()

    def own_rows(self, which, along):
        height = self.sides[which].shape[2]
        place = self.links.at(along, self.links.across)
        return pl.ds(pl.multiple_of(place * height, 16), height)

    def across_sum(self, which, along):
        total = self.sums[which][self.own_rows(which, along), :].astype(jnp.float32)
        for step in range(1, self.links.across_count):
            self.side_copy(which, step, along).wait_recv()
            total = total + self.sides[which][step - 1, along].astype(jnp.float32)
        return total

    def pass_on(self, distance):
        links = self.links
        last = links.along_count - 1
        for which in (1, 0):
            for way in range(2):
                if way == 0:
                    present = links.along + distance <= last
                    along = jnp.minimum(links.along + distance, last)
                    behind = links.along > 0
                else:
                    present = links.along >= distance
                    along = jnp.maximum(links.along - distance, 0)
                    behind = links.along < last

                @pl.when(present)
                def _():
                    rows = self.own_rows(which, along)
                    self.sums[which][rows, :] = self.across_sum(which, along).astype(jnp.bfloat16)

                    @pl.when(behind)
                    def _():
                        self.line_copy(which, way, along).wait_recv()
                        more = self.lines[which][way, along].astype(jnp.float32)
                        total = self.sums[which][rows, :].astype(jnp.float32) + more
                        self.sums[which][rows, :] = total.astype(jnp.bfloat16)

                    self.line_copy(which, way, along).start()

    def finish(self, outputs):
        links = self.links
        for which in (1, 0):
            outputs[which][...] = self.across_sum(which, links.along)
            for way in range(2):
                behind = links.along > 0 if way == 0 else links.along < links.along_count - 1

                @pl.when(behind)
                def _():
                    self.line_copy(which, way, links.along).wait_recv()
                    outputs[which][...] += self.lines[which][way, links.along].astype(jnp.float32)

    def wait_sends(self):
        links = self.links
        for which in range(2):
            for along in range(links.along_count):
                for step in range(1, links.across_count):
                    self.side_copy(which, step, along).wait_send()

                @pl.when(along > links.along)
                def _():
                    self.line_copy(which, 0, along).wait_send()

                @pl.when(along < links.along)
                def _():
                    self.line_copy(which, 1, along).wait_send()


def kernel(
    section_count, group_count, across_count, micro_count, slots, inside,
    x_ref, target_ref, live_ref, taps_ref, own_first, own_second, head_ref,
    grad_in_ref, grad_out_ref, small_ref,
    tiles, results, ups, tile_grads, mixed, normed, normed_low, inverse, activated, slope,
    hidden_grad, kernel_acc, head_block,
    tile_send, tile_recv, up_send, up_recv, head_send, head_recv,
    *more,
):
    section = lax.axis_index("section")
    last = section_count - 1
    cells = slots * SIDE * SIDE
    width = x_ref.shape[-1]
    expand = own_first.shape[1]
    lane_tiles = width // LANES
    is_first = section == 0
    is_last = section == last
    following = jnp.minimum(section + 1, last)
    previous = jnp.maximum(section - 1, 0)

    barrier = pltpu.get_barrier_semaphore()
    for step in range(1, section_count):
        peer = lax.rem(section + step, section_count)
        pl.semaphore_signal(barrier, inc=1, device_id={"section": peer}, device_id_type=MESH)
    if inside:
        group = lax.axis_index("dp")
        for step in range(1, group_count):
            peer = lax.rem(group + step, group_count)
            pl.semaphore_signal(barrier, inc=1, device_id={"dp": peer}, device_id_type=MESH)
    pl.semaphore_wait(barrier, section_count - 1 + (group_count - 1 if inside else 0))

    if inside:
        (
            first_ref, second_ref, sum_in, sum_out, side_in, side_out, line_in, line_out,
            stage, landed, gather_recv, gather_line, gather_side,
            side_send, side_recv, line_send, line_recv, small_send, small_recv,
        ) = more
        links = Links(group, group_count, across_count)
        weights = ((own_first, first_ref), (own_second, second_ref))
        gather(links, weights, gather_recv, gather_line, gather_side)
    else:
        first_ref, second_ref, sum_in, sum_out = own_first, own_second, grad_in_ref, grad_out_ref

    def rows_of(micro):
        return pl.ds(pl.multiple_of(micro * cells, cells), cells)

    def tile_copy(micro):
        return pltpu.make_async_remote_copy(
            src_ref=results.at[micro], dst_ref=tiles.at[micro],
            send_sem=tile_send.at[micro], recv_sem=tile_recv.at[micro],
            device_id={"section": following}, device_id_type=MESH,
        )

    def up_copy(micro):
        return pltpu.make_async_remote_copy(
            src_ref=tile_grads.at[micro], dst_ref=ups.at[micro],
            send_sem=up_send.at[micro], recv_sem=up_recv.at[micro],
            device_id={"section": previous}, device_id_type=MESH,
        )

    def head_copy(step):
        peer = lax.rem(section + step, section_count)
        return pltpu.make_async_remote_copy(
            src_ref=head_block, dst_ref=head_block,
            send_sem=head_send.at[step - 1], recv_sem=head_recv,
            device_id={"section": peer}, device_id_type=MESH,
        )

    @pl.when(is_last)
    def _():
        head_block[...] = jnp.zeros_like(head_block)

    def forward(micro, carry):
        @pl.when(is_first)
        def _():
            tiles[micro] = x_ref[micro]

        @pl.when(jnp.logical_not(is_first))
        def _():
            tile_copy(micro).wait_recv()

        def mix(index, carry):
            lanes = lane_tile(index)
            values = tiles[micro, :, lanes].astype(jnp.float32)
            values = values.reshape(slots, SIDE, SIDE, LANES)
            mixed[:, lanes] = depthwise(values, taps_ref, lanes, False).reshape(cells, LANES)
            return carry

        lax.fori_loop(0, lane_tiles, mix, 0)
        rows = rows_of(micro)
        value = mixed[...]
        centred = value - jnp.mean(value, axis=-1, keepdims=True)
        scale = lax.rsqrt(jnp.mean(centred * centred, axis=-1, keepdims=True) + EPSILON)
        unit = centred * scale
        low = unit.astype(jnp.bfloat16)
        normed[rows, :] = unit
        normed_low[rows, :] = low
        inverse[rows, :] = jnp.broadcast_to(scale, (cells, LANES))
        total = tiles[micro].astype(jnp.float32)
        for start in range(0, expand, CHUNK):
            columns = slice(start, start + CHUNK)
            hidden = jnp.dot(low, first_ref[:, columns], preferred_element_type=jnp.float32)
            portion = 0.5 * (1.0 + lax.erf(hidden * SQRT_HALF))
            active = (hidden * portion).astype(jnp.bfloat16)
            activated[rows, columns] = active
            slope[rows, columns] = (
                portion + hidden * jnp.exp(-0.5 * hidden * hidden) * INV_ROOT_TWO_PI
            )
            total = total + jnp.dot(
                active, second_ref[columns, :], preferred_element_type=jnp.float32
            )
        results[micro] = total.astype(jnp.bfloat16)

        @pl.when(jnp.logical_not(is_last))
        def _():
            tile_copy(micro).start()

        @pl.when(is_last)
        def _():
            final = results[micro].astype(jnp.float32)
            logits = jnp.sum(final * head_ref[...], axis=-1, keepdims=True)
            weight = live_ref[micro]
            truth = target_ref[micro]
            factor = 1.0 / (micro_count * slots)
            softplus = jnp.maximum(logits, 0.0) + jnp.log1p(jnp.exp(-jnp.abs(logits)))
            loss = jnp.sum(weight * (softplus - truth * logits)) * factor
            logit_grad = (1.0 / (1.0 + jnp.exp(-logits)) - truth) * weight * factor
            ups[micro] = (logit_grad * head_ref[...]).astype(jnp.bfloat16)
            term = jnp.sum(logit_grad * final, axis=0, keepdims=True)
            head_block[0:1, :] += term
            head_block[1:2, :] += jnp.full((1, width), loss)

        return carry

    lax.fori_loop(0, micro_count, forward, 0)

    @pl.when(is_last)
    def _():
        for step in range(1, section_count):
            head_copy(step).start()

    def backward(micro, carry):
        @pl.when(jnp.logical_not(is_last))
        def _():
            up_copy(micro).wait_recv()

        rows = rows_of(micro)
        upstream = ups[micro]
        total = jnp.zeros((cells, width), jnp.float32)
        for start in range(0, expand, CHUNK):
            columns = slice(start, start + CHUNK)
            through = lax.dot_general(
                upstream, second_ref[columns, :], (((1,), (1,)), ((), ())),
                preferred_element_type=jnp.float32,
            )
            grad = (through * slope[rows, columns]).astype(jnp.bfloat16)
            hidden_grad[rows, columns] = grad
            total = total + lax.dot_general(
                grad, first_ref[:, columns], (((1,), (1,)), ((), ())),
                preferred_element_type=jnp.float32,
            )
        unit = normed[rows, :]
        mixed_grad = inverse[rows, 0:1] * (
            total
            - jnp.mean(total, axis=-1, keepdims=True)
            - unit * jnp.mean(total * unit, axis=-1, keepdims=True)
        )
        normed[rows, :] = mixed_grad

        def unmix(index, carry):
            lanes = lane_tile(index)
            values = normed[rows, lanes].reshape(slots, SIDE, SIDE, LANES)
            back = depthwise(values, taps_ref, lanes, True).reshape(cells, LANES)
            back = back + ups[micro, :, lanes].astype(jnp.float32)
            tile_grads[micro, :, lanes] = back.astype(jnp.bfloat16)
            return carry

        @pl.when(jnp.logical_not(is_first))
        def _():
            lax.fori_loop(0, lane_tiles, unmix, 0)
            up_copy(micro).start()

        return carry

    lax.fori_loop(0, micro_count, backward, 0)

    upstreams = ups[...].reshape(micro_count * cells, width)
    parts = expand // LANES // lane_tiles
    if inside:
        parts = links.along_count
        scatter = Scatter(
            links, (sum_in, sum_out), (side_in, side_out), (line_in, line_out),
            side_send, side_recv, line_send, line_recv,
        )
    step_columns = expand // parts

    def out_part(turn, carry):
        part = links.far_first(turn) if inside else turn
        columns = pl.ds(pl.multiple_of(part * step_columns, LANES), step_columns)
        sum_out[columns, :] = lax.dot_general(
            activated[:, columns], upstreams, (((0,), (0,)), ((), ())),
            preferred_element_type=jnp.float32,
        ).astype(jnp.bfloat16)
        if inside:
            scatter.start_side(1, part)
        return carry

    lax.fori_loop(0, parts, out_part, 0)
    for start in range(0, expand, CHUNK):
        columns = slice(start, start + CHUNK)
        sum_in[:, columns] = lax.dot_general(
            normed_low[...], hidden_grad[:, columns], (((0,), (0,)), ((), ())),
            preferred_element_type=jnp.float32,
        ).astype(jnp.bfloat16)
    if inside:
        for turn in range(parts):
            scatter.start_side(0, links.far_first(turn))

    kernel_acc[...] = jnp.zeros_like(kernel_acc)

    def tap_grads(flat, carry):
        micro = flat // lane_tiles
        lanes = lane_tile(flat % lane_tiles)
        values = tiles[micro, :, lanes].astype(jnp.float32)
        values = values.reshape(slots, SIDE, SIDE, LANES)
        grads = normed[rows_of(micro), lanes].reshape(slots, SIDE, SIDE, LANES)
        for across in range(TAPS):
            shifted = shift_columns(values, across - 3)
            for vertical in range(TAPS):
                offset = vertical - 3
                low, high = max(0, -offset), min(SIDE, SIDE - offset)
                product = shifted[:, low + offset : high + offset] * grads[:, low:high]
                kernel_acc[vertical * TAPS + across, :, lanes] += jnp.sum(product, axis=(0, 1))
        return carry

    lax.fori_loop(0, micro_count * lane_tiles, tap_grads, 0)
    small = stage.at[0] if inside else small_ref
    small[0:HEAD_ROW, :] = jnp.sum(kernel_acc[...], axis=1)

    @pl.when(is_last)
    def _():
        for step in range(1, section_count):
            head_copy(step).wait_send()

    @pl.when(jnp.logical_not(is_last))
    def _():
        head_copy(1).wait_recv()

    small[HEAD_ROW:SMALL_ROWS, :] = head_block[...]
    if inside:
        rounds = stage.shape[0] - 1

        def small_copy(turn):
            weight = 1 << turn
            bit = lax.rem(group // weight, 2)
            return pltpu.make_async_remote_copy(
                src_ref=stage.at[turn], dst_ref=landed.at[turn],
                send_sem=small_send.at[turn], recv_sem=small_recv.at[turn],
                device_id={"dp": group + weight * (1 - 2 * bit)}, device_id_type=MESH,
            )

        def small_round(turn):
            if turn < rounds:
                small_copy(turn).wait()
                stage[turn + 1] = stage[turn] + landed[turn]
                if turn + 1 < rounds:
                    small_copy(turn + 1).start()

        small_copy(0).start()
        level = 0
        for distance in range(links.along_count - 1, 0, -1):
            scatter.pass_on(distance)
            small_round(level)
            level += 1
        scatter.finish((grad_in_ref, grad_out_ref))
        for turn in range(level, rounds):
            small_round(turn)
        small_ref[...] = stage[rounds]
        scatter.wait_sends()
        wait_gather_sends(links, weights, gather_recv, gather_line, gather_side)

    def finish(micro, carry):
        @pl.when(jnp.logical_not(is_last))
        def _():
            tile_copy(micro).wait_send()

        @pl.when(jnp.logical_not(is_first))
        def _():
            up_copy(micro).wait_send()

        return carry

    lax.fori_loop(0, micro_count, finish, 0)


def body(crop_maps, target_maps, crop_counts, depth_kernels, weight_in, weight_out, head_weight):
    section_count = lax.axis_size("section")
    micro_count, slots = crop_maps.shape[1:3]
    width = crop_maps.shape[-1]
    cells = slots * SIDE * SIDE
    expand = weight_in.shape[2]
    live = jnp.arange(slots)[None, :] < crop_counts[0][:, None]
    entering = crop_maps[0] * live[:, :, None, None, None].astype(jnp.bfloat16)
    entering = entering.reshape(micro_count, cells, width)
    targets = target_maps[0].reshape(micro_count, cells, 1).astype(jnp.float32)
    weights = jnp.broadcast_to(
        live[:, :, None].astype(jnp.float32), (micro_count, slots, SIDE * SIDE)
    ).reshape(micro_count, cells, 1)
    group_count = lax.axis_size("dp")
    height_in, height_out = weight_in.shape[1], weight_out.shape[1]
    across_count = 1
    while 4 * across_count * across_count <= group_count:
        across_count *= 2
    along_count = group_count // across_count
    rounds = group_count.bit_length() - 1
    inside = (
        height_in % 16 == 0
        and height_out % 16 == 0
        and group_count == 1 << rounds
        and group_count > 1
        and across_count * height_out % LANES == 0
    )
    first, second = weight_in[0], weight_out[0]
    if not inside:
        first = lax.all_gather(first, "dp", axis=0, tiled=True)
        second = lax.all_gather(second, "dp", axis=0, tiled=True)
    low, full = jnp.bfloat16, jnp.float32
    every = micro_count * cells
    in_vmem = pl.BlockSpec(memory_space=pltpu.VMEM)
    shapes = [
        ((height_in, expand), full) if inside else ((width, expand), low),
        ((height_out, width), full) if inside else ((expand, width), low),
        ((SMALL_ROWS, width), full),
    ]
    scratch = [
        pltpu.VMEM((micro_count, cells, width), low),
        pltpu.VMEM((micro_count, cells, width), low),
        pltpu.VMEM((micro_count, cells, width), low),
        pltpu.VMEM((micro_count, cells, width), low),
        pltpu.VMEM((cells, width), full),
        pltpu.VMEM((every, width), full),
        pltpu.VMEM((every, width), low),
        pltpu.VMEM((every, LANES), full),
        pltpu.VMEM((every, expand), low),
        pltpu.VMEM((every, expand), full),
        pltpu.VMEM((every, expand), low),
        pltpu.VMEM((HEAD_ROW, SIDE, width), full),
        pltpu.VMEM((SMALL_ROWS - HEAD_ROW, width), full),
        pltpu.SemaphoreType.DMA((micro_count,)),
        pltpu.SemaphoreType.DMA((micro_count,)),
        pltpu.SemaphoreType.DMA((micro_count,)),
        pltpu.SemaphoreType.DMA((micro_count,)),
        pltpu.SemaphoreType.DMA((section_count - 1,)),
        pltpu.SemaphoreType.DMA,
    ]
    if inside:
        sides = across_count - 1
        scratch += [
            pltpu.VMEM((width, expand), low),
            pltpu.VMEM((expand, width), low),
            pltpu.VMEM((width, expand), low),
            pltpu.VMEM((expand, width), low),
            pltpu.VMEM((sides, along_count, height_in, expand), low),
            pltpu.VMEM((sides, along_count, height_out, width), low),
            pltpu.VMEM((2, along_count, height_in, expand), low),
            pltpu.VMEM((2, along_count, height_out, width), low),
            pltpu.VMEM((rounds + 1, SMALL_ROWS, width), full),
            pltpu.VMEM((rounds, SMALL_ROWS, width), full),
            pltpu.SemaphoreType.DMA((2, group_count)),
            pltpu.SemaphoreType.DMA((2, 2, along_count)),
            pltpu.SemaphoreType.DMA((2, sides, along_count)),
            pltpu.SemaphoreType.DMA((2, sides, along_count)),
            pltpu.SemaphoreType.DMA((2, sides, along_count)),
            pltpu.SemaphoreType.DMA((2, 2, along_count)),
            pltpu.SemaphoreType.DMA((2, 2, along_count)),
            pltpu.SemaphoreType.DMA((rounds,)),
            pltpu.SemaphoreType.DMA((rounds,)),
        ]
    grad_in, grad_out, small = pl.pallas_call(
        functools.partial(
            kernel, section_count, group_count, across_count, micro_count, slots, inside
        ),
        out_shape=tuple(jax.ShapeDtypeStruct(shape, kind) for shape, kind in shapes),
        in_specs=[in_vmem] * 7,
        out_specs=(in_vmem,) * 3,
        scratch_shapes=scratch,
        compiler_params=pltpu.CompilerParams(
            collective_id=0, has_side_effects=True, vmem_limit_bytes=60 * 1024 * 1024
        ),
        cost_estimate=pl.CostEstimate(
            flops=12 * every * width * expand, bytes_accessed=8 * width * expand, transcendentals=0
        ),
    )(entering, targets, weights, depth_kernels[0], first, second, head_weight[None])
    if not inside:
        grad_in = lax.psum_scatter(grad_in, "dp", scatter_dimension=0, tiled=True).astype(full)
        grad_out = lax.psum_scatter(grad_out, "dp", scatter_dimension=0, tiled=True).astype(full)
        small = lax.psum(small, "dp")
    taps = depth_kernels.shape[1]
    return (
        grad_in[None],
        grad_out[None],
        small[:taps][None],
        small[HEAD_ROW],
        small[HEAD_ROW + 1, 0],
    )


def solution(mesh):
    return jax.shard_map(
        body,
        mesh=mesh,
        in_specs=(
            P("dp", None, None, None, None, None),
            P("dp", None, None, None, None),
            P("dp", None),
            P("section", None, None),
            P("section", "dp", None),
            P("section", "dp", None),
            P(),
        ),
        out_specs=(
            P("section", "dp", None),
            P("section", "dp", None),
            P("section", None, None),
            P(),
            P(),
        ),
        check_vma=False,
    )
```

```python
import functools

import jax
import jax.numpy as jnp
from jax import lax
from jax.experimental import pallas as pl
from jax.experimental.pallas import tpu as pltpu
from jax.sharding import PartitionSpec as P

EPSILON = 1e-06
SQRT_HALF = 0.7071067811865476
INV_ROOT_TWO_PI = 0.3989422804014327
MESH = pl.DeviceIdType.MESH
LANES = 128
CHUNK = 512
TAPS = 7
SIDE = 8
SMALL_ROWS = 64
HEAD_ROW = 56


def shift_columns(values, distance):
    if distance == 0:
        return values
    column = lax.broadcasted_iota(jnp.int32, values.shape, 2)
    moved = pltpu.roll(values, (-distance) % SIDE, 2)
    keep = (column + distance >= 0) & (column + distance < SIDE)
    return jnp.where(keep, moved, 0.0)


def valid_rows(offset):
    return range(max(0, -offset), min(SIDE, SIDE - offset))


def depthwise(values, taps_ref, lanes, flip):
    rows = [jnp.zeros_like(values[:, 0]) for _ in range(SIDE)]
    for across in range(TAPS):
        shifted = shift_columns(values, across - 3)
        for vertical in range(TAPS):
            tap = vertical * TAPS + across
            if flip:
                tap = TAPS * TAPS - 1 - tap
            weight = taps_ref[pl.ds(tap, 1), lanes].reshape(1, 1, LANES)
            for row in valid_rows(vertical - 3):
                rows[row] = rows[row] + shifted[:, row + vertical - 3] * weight
    return jnp.stack(rows, axis=1)


def lane_tile(index):
    return pl.ds(pl.multiple_of(index * LANES, LANES), LANES)


class Place:
    def __init__(self):
        group, self.home = lax.axis_index("dp"), lax.axis_index("section")
        self.group = group
        self.along, self.across = group // 2, lax.rem(group, 2)
        self.row, self.core = self.home // 2, lax.rem(self.home, 2)
        self.role = self.swap(self.along)
        self.role_row, self.role_core = lax.rem(self.along, 2), self.along // 2
        self.keeper = self.home == self.role

    def swap(self, index):
        return 2 * lax.rem(index, 2) + index // 2

    def at(self, along=None, across=None, row=None, core=None):
        along = self.along if along is None else along
        across = self.across if across is None else across
        row = self.row if row is None else row
        core = self.core if core is None else core
        return {"dp": 2 * along + across, "section": 2 * row + core}

    def near_first(self, turn):
        return jnp.where(
            self.along < 2, lax.rem(self.along + turn, 4), lax.rem(self.along - turn + 4, 4)
        )

    def far_first(self, turn):
        return jnp.where(self.along < 2, 3 - turn, turn)


def remote(source, target, send_sem, recv_sem, device):
    return pltpu.make_async_remote_copy(
        src_ref=source, dst_ref=target, send_sem=send_sem, recv_sem=recv_sem,
        device_id=device, device_id_type=MESH,
    )


def slab(ref, place, height):
    return ref.at[pl.ds(pl.multiple_of(place * height, 16), height), :]


class Gather:
    def __init__(self, place, weights, recv, first_send, core_send, across_send, row_send):
        self.place, self.weights, self.recv = place, weights, recv
        self.first_send, self.core_send = first_send, core_send
        self.across_send, self.row_send = across_send, row_send

    def shard(self, which, origin):
        own, full = self.weights[which]
        return slab(full, origin, own.shape[0])

    def launch(self, which):
        place = self.place
        plane = place.swap(place.home)
        target = self.shard(which, place.group)
        return remote(
            self.weights[which][0], target, self.first_send.at[which],
            self.recv.at[which, place.group], place.at(along=plane, core=which),
        )

    def stays(self, which):
        return self.place.keeper & (self.place.core == which)

    def spread(self, which, origin, sem, device):
        target = self.shard(which, origin)
        return remote(target, target, sem, self.recv.at[which, origin], device)

    def to_core(self, which, origin):
        place = self.place
        return self.spread(
            which, origin, self.core_send.at[origin], place.at(core=1 - place.core)
        )

    def to_across(self, which, along):
        place = self.place
        return self.spread(
            which, 2 * along + place.across, self.across_send.at[along],
            place.at(across=1 - place.across),
        )

    def to_row(self, which, along):
        place = self.place
        return self.spread(
            which, 2 * along + place.across, self.row_send.at[along], place.at(row=1 - place.row)
        )

    def start(self):
        for which in range(2):
            stays = self.stays(which)

            @pl.when(jnp.logical_not(stays))
            def _():
                self.launch(which).start()

            @pl.when(stays)
            def _():
                own, full = self.weights[which]
                height = own.shape[0]
                start = pl.multiple_of(self.place.group * height, 16)
                full[pl.ds(start, height), :] = own[...]

    def run(self):
        place = self.place
        in_row = place.row == place.role_row
        for which in range(2):

            @pl.when(place.core == which)
            def _():
                for turn in range(4):
                    along = place.near_first(turn)
                    origin = 2 * along + place.across
                    if turn == 0:

                        @pl.when(jnp.logical_not(place.keeper))
                        def _():
                            self.to_core(which, origin).wait_recv()
                    else:
                        self.to_core(which, origin).wait_recv()
                    self.to_across(which, along).start()

                    @pl.when(in_row)
                    def _():
                        self.to_row(which, along).start()

                    self.to_core(which, origin).start()
                for turn in range(4):
                    origin = 2 * place.near_first(turn) + 1 - place.across
                    self.to_core(which, origin).wait_recv()
                    self.to_core(which, origin).start()

        for which in range(2):

            @pl.when(place.core != which)
            def _():
                for origin in range(8):
                    self.to_core(which, origin).wait_recv()

    def wait_sends(self):
        place = self.place
        for which in range(2):

            @pl.when(jnp.logical_not(self.stays(which)))
            def _():
                self.launch(which).wait_send()

            @pl.when(place.core == which)
            def _():
                for along in range(4):
                    self.to_across(which, along).wait_send()

                    @pl.when(place.row == place.role_row)
                    def _():
                        self.to_row(which, along).wait_send()

                for origin in range(8):
                    self.to_core(which, origin).wait_send()


class Scatter:
    def __init__(self, place, sums, cores, sides, rows, homes, sems):
        self.place, self.sums, self.cores = place, sums, cores
        self.sides, self.rows, self.homes = sides, rows, homes
        (
            self.core_send, self.core_recv, self.side_send, self.side_recv,
            self.row_send, self.row_recv, self.home_send, self.home_recv,
        ) = sems

    def height(self, which):
        return self.sides[which].shape[1]

    def core_copy(self, which, along):
        place, height = self.place, 2 * self.height(which)
        return remote(
            slab(self.sums[which], along, height), slab(self.cores[which], along, height),
            self.core_send.at[along], self.core_recv.at[along], place.at(core=1 - place.core),
        )

    def side_copy(self, which, along):
        place = self.place
        source = slab(self.sums[which], 2 * along + 1 - place.across, self.height(which))
        return remote(
            source, self.sides[which].at[along], self.side_send.at[along],
            self.side_recv.at[along], place.at(across=1 - place.across),
        )

    def row_copy(self, which, along):
        place = self.place
        source = slab(self.sums[which], 2 * along + place.across, self.height(which))
        return remote(
            source, self.rows[which].at[along], self.row_send.at[along],
            self.row_recv.at[along], place.at(row=1 - place.row),
        )

    def home_copy(self, which, along):
        place = self.place
        source = slab(self.sums[which], 2 * along + place.across, self.height(which))
        return remote(
            source, self.homes[which], self.home_send.at[along], self.home_recv.at[which],
            place.at(along=along, core=place.role_core),
        )

    def goes(self, along):
        place = self.place
        return (along != place.along) | (place.core != place.role_core)

    def add(self, which, along, count, first, buffer):
        height = count * self.height(which)
        start = pl.multiple_of(first * self.height(which), 16)
        rows = pl.ds(start, height)
        total = self.sums[which][rows, :].astype(jnp.float32) + buffer.astype(jnp.float32)
        self.sums[which][rows, :] = total.astype(jnp.bfloat16)

    def give_core(self, which, along):
        @pl.when(self.place.core != which)
        def _():
            self.core_copy(which, along).start()

    def over_core(self, turn):
        along = self.place.far_first(turn)
        for which in range(2):

            @pl.when(self.place.core == which)
            def _():
                self.core_copy(which, along).wait_recv()
                height = 2 * self.height(which)
                start = pl.multiple_of(along * height, 16)
                self.add(which, along, 2, 2 * along, self.cores[which][pl.ds(start, height), :])
                self.side_copy(which, along).start()

    def over_plane(self, turn):
        place = self.place
        along = place.far_first(turn)
        in_row = place.row == place.role_row
        for which in range(2):

            @pl.when(place.core == which)
            def _():
                self.side_copy(which, along).wait_recv()
                own = 2 * along + place.across
                self.add(which, along, 1, own, self.sides[which][along])

                @pl.when(jnp.logical_not(in_row))
                def _():
                    self.row_copy(which, along).start()

                @pl.when(in_row)
                def _():
                    self.row_copy(which, along).wait_recv()
                    self.add(which, along, 1, own, self.rows[which][along])

                    @pl.when(self.goes(along))
                    def _():
                        self.home_copy(which, along).start()

                    @pl.when(jnp.logical_not(self.goes(along)))
                    def _():
                        height = self.height(which)
                        start = pl.multiple_of(own * height, 16)
                        self.homes[which][...] = self.sums[which][pl.ds(start, height), :]

    def finish(self, outputs):
        place = self.place
        for which in range(2):
            here = place.keeper & (place.core == which)

            @pl.when(jnp.logical_not(here))
            def _():
                self.home_copy(which, 0).wait_recv()

            outputs[which][...] = self.homes[which][...].astype(jnp.float32)

    def wait_sends(self):
        place = self.place
        in_row = place.row == place.role_row
        for which in range(2):
            for along in range(4):

                @pl.when(place.core != which)
                def _():
                    self.core_copy(which, along).wait_send()

                @pl.when(place.core == which)
                def _():
                    self.side_copy(which, along).wait_send()

                    @pl.when(jnp.logical_not(in_row))
                    def _():
                        self.row_copy(which, along).wait_send()

                    @pl.when(in_row & self.goes(along))
                    def _():
                        self.home_copy(which, along).wait_send()


def kernel(
    section_count, micro_count, slots, inside,
    x_ref, own_labels, own_taps, own_first, own_second, head_ref,
    grad_in_ref, grad_out_ref, small_ref,
    tiles, results, ups, tile_grads, mixed, normed, normed_low, inverse, activated, slope,
    hidden_grad, kernel_acc, head_block,
    tile_send, tile_recv, up_send, up_recv, head_send, head_recv,
    *more,
):
    last = section_count - 1
    if inside:
        place = Place()
        section = place.role
        peers = [place.at(along=lax.rem(place.along + step, 4)) for step in range(1, 4)]
        peers += [
            place.at(along=lax.rem(place.along + step, 4), core=1 - place.core)
            for step in range(4)
        ]
        peers += [place.at(row=1 - place.row)]
        peers += [place.at(row=1 - place.row, core=1 - place.core)]
        peers += [place.at(across=1 - place.across)]
    else:
        section = lax.axis_index("section")
        peers = [
            {"section": lax.rem(section + step, section_count)} for step in range(1, section_count)
        ]
    cells = slots * SIDE * SIDE
    width = x_ref.shape[-1]
    expand = own_first.shape[1]
    lane_tiles = width // LANES
    is_first = section == 0
    is_last = section == last
    following = jnp.minimum(section + 1, last)
    previous = jnp.maximum(section - 1, 0)

    def worker(index):
        return place.at(along=place.swap(index)) if inside else {"section": index}

    barrier = pltpu.get_barrier_semaphore()
    for peer in peers:
        pl.semaphore_signal(barrier, inc=1, device_id=peer, device_id_type=MESH)
    pl.semaphore_wait(barrier, len(peers))

    if inside:
        (
            first_ref, second_ref, sum_in, sum_out, core_in, core_out, side_in, side_out,
            row_in, row_out, home_in, home_out, stage, landed, home_small, taps_ref, labels,
            gather_recv, launch_send, spread_core, spread_across, spread_row,
            core_send, core_recv, side_send, side_recv, row_send, row_recv, home_send, home_recv,
            small_send, small_recv, back_send, back_recv, crop_send, label_send, label_recv,
            taps_send, taps_recv,
        ) = more
        is_source = place.along == place.home

        def crop_copy(micro):
            return remote(
                x_ref.at[micro], tiles.at[micro], crop_send.at[micro], tile_recv.at[micro],
                place.at(along=0),
            )

        label_copy = remote(own_labels, labels, label_send, label_recv, place.at(along=3))

        def taps_copy(step):
            device = {"dp": place.group, "section": lax.rem(place.home + step, 4)}
            return remote(own_taps, taps_ref, taps_send.at[step - 1], taps_recv, device)

        gather = Gather(
            place, ((own_first, first_ref), (own_second, second_ref)),
            gather_recv, launch_send, spread_core, spread_across, spread_row,
        )
        gather.start()

        @pl.when(place.keeper)
        def _():
            for step in range(1, 4):
                taps_copy(step).start()
            taps_ref[...] = own_taps[...]

        @pl.when(is_source & (place.along != 0))
        def _():
            for micro in range(micro_count):
                crop_copy(micro).start()

        @pl.when(is_source & (place.along != 3))
        def _():
            label_copy.start()

        @pl.when(is_source & (place.along == 3))
        def _():
            labels[...] = own_labels[...]

        gather.run()

        @pl.when(jnp.logical_not(place.keeper))
        def _():
            taps_copy(1).wait_recv()

        @pl.when((place.along == 3) & jnp.logical_not(is_source))
        def _():
            label_copy.wait_recv()

        own_crops = is_first & (place.home == 0)
    else:
        first_ref, second_ref, sum_in, sum_out = own_first, own_second, grad_in_ref, grad_out_ref
        taps_ref, labels, own_crops = own_taps, own_labels, is_first

    def rows_of(micro):
        return pl.ds(pl.multiple_of(micro * cells, cells), cells)

    def tile_copy(micro):
        return pltpu.make_async_remote_copy(
            src_ref=results.at[micro], dst_ref=tiles.at[micro],
            send_sem=tile_send.at[micro], recv_sem=tile_recv.at[micro],
            device_id=worker(following), device_id_type=MESH,
        )

    def up_copy(micro):
        return pltpu.make_async_remote_copy(
            src_ref=tile_grads.at[micro], dst_ref=ups.at[micro],
            send_sem=up_send.at[micro], recv_sem=up_recv.at[micro],
            device_id=worker(previous), device_id_type=MESH,
        )

    def head_copy(step):
        peer = lax.rem(section + step, section_count)
        return pltpu.make_async_remote_copy(
            src_ref=head_block, dst_ref=head_block,
            send_sem=head_send.at[step - 1], recv_sem=head_recv,
            device_id=worker(peer), device_id_type=MESH,
        )

    @pl.when(is_last)
    def _():
        head_block[...] = jnp.zeros_like(head_block)

    def forward(micro, carry):
        @pl.when(own_crops)
        def _():
            tiles[micro] = x_ref[micro]

        @pl.when(jnp.logical_not(own_crops))
        def _():
            tile_copy(micro).wait_recv()

        def mix(index, carry):
            lanes = lane_tile(index)
            values = tiles[micro, :, lanes].astype(jnp.float32)
            values = values.reshape(slots, SIDE, SIDE, LANES)
            mixed[:, lanes] = depthwise(values, taps_ref, lanes, False).reshape(cells, LANES)
            return carry

        lax.fori_loop(0, lane_tiles, mix, 0)
        rows = rows_of(micro)
        value = mixed[...]
        centred = value - jnp.mean(value, axis=-1, keepdims=True)
        scale = lax.rsqrt(jnp.mean(centred * centred, axis=-1, keepdims=True) + EPSILON)
        unit = centred * scale
        low = unit.astype(jnp.bfloat16)
        normed[rows, :] = unit
        normed_low[rows, :] = low
        inverse[rows, :] = jnp.broadcast_to(scale, (cells, LANES))
        total = tiles[micro].astype(jnp.float32)
        for start in range(0, expand, CHUNK):
            columns = slice(start, start + CHUNK)
            hidden = jnp.dot(low, first_ref[:, columns], preferred_element_type=jnp.float32)
            portion = 0.5 * (1.0 + lax.erf(hidden * SQRT_HALF))
            active = (hidden * portion).astype(jnp.bfloat16)
            activated[rows, columns] = active
            slope[rows, columns] = (
                portion + hidden * jnp.exp(-0.5 * hidden * hidden) * INV_ROOT_TWO_PI
            )
            total = total + jnp.dot(
                active, second_ref[columns, :], preferred_element_type=jnp.float32
            )
        results[micro] = total.astype(jnp.bfloat16)

        @pl.when(jnp.logical_not(is_last))
        def _():
            tile_copy(micro).start()

        @pl.when(is_last)
        def _():
            final = results[micro].astype(jnp.float32)
            logits = jnp.sum(final * head_ref[...], axis=-1, keepdims=True)
            truth = labels[micro, :, 0:1]
            weight = labels[micro, :, 1:2]
            factor = 1.0 / (micro_count * slots)
            softplus = jnp.maximum(logits, 0.0) + jnp.log1p(jnp.exp(-jnp.abs(logits)))
            loss = jnp.sum(weight * (softplus - truth * logits)) * factor
            logit_grad = (1.0 / (1.0 + jnp.exp(-logits)) - truth) * weight * factor
            ups[micro] = (logit_grad * head_ref[...]).astype(jnp.bfloat16)
            term = jnp.sum(logit_grad * final, axis=0, keepdims=True)
            head_block[0:1, :] += term
            head_block[1:2, :] += jnp.full((1, width), loss)

        return carry

    lax.fori_loop(0, micro_count, forward, 0)

    @pl.when(is_last)
    def _():
        for step in range(1, section_count):
            head_copy(step).start()

    def backward(micro, carry):
        @pl.when(jnp.logical_not(is_last))
        def _():
            up_copy(micro).wait_recv()

        rows = rows_of(micro)
        upstream = ups[micro]
        total = jnp.zeros((cells, width), jnp.float32)
        for start in range(0, expand, CHUNK):
            columns = slice(start, start + CHUNK)
            through = lax.dot_general(
                upstream, second_ref[columns, :], (((1,), (1,)), ((), ())),
                preferred_element_type=jnp.float32,
            )
            grad = (through * slope[rows, columns]).astype(jnp.bfloat16)
            hidden_grad[rows, columns] = grad
            total = total + lax.dot_general(
                grad, first_ref[:, columns], (((1,), (1,)), ((), ())),
                preferred_element_type=jnp.float32,
            )
        unit = normed[rows, :]
        mixed_grad = inverse[rows, 0:1] * (
            total
            - jnp.mean(total, axis=-1, keepdims=True)
            - unit * jnp.mean(total * unit, axis=-1, keepdims=True)
        )
        normed[rows, :] = mixed_grad

        def unmix(index, carry):
            lanes = lane_tile(index)
            values = normed[rows, lanes].reshape(slots, SIDE, SIDE, LANES)
            back = depthwise(values, taps_ref, lanes, True).reshape(cells, LANES)
            back = back + ups[micro, :, lanes].astype(jnp.float32)
            tile_grads[micro, :, lanes] = back.astype(jnp.bfloat16)
            return carry

        @pl.when(jnp.logical_not(is_first))
        def _():
            lax.fori_loop(0, lane_tiles, unmix, 0)
            up_copy(micro).start()

        return carry

    lax.fori_loop(0, micro_count, backward, 0)

    upstreams = ups[...].reshape(micro_count * cells, width)
    parts = expand // LANES // lane_tiles
    if inside:
        parts = 4
        scatter = Scatter(
            place, (sum_in, sum_out), (core_in, core_out), (side_in, side_out),
            (row_in, row_out), (home_in, home_out),
            (
                core_send, core_recv, side_send, side_recv,
                row_send, row_recv, home_send, home_recv,
            ),
        )
    step_columns = expand // parts

    def out_part(turn, carry):
        part = place.far_first(turn) if inside else turn
        columns = pl.ds(pl.multiple_of(part * step_columns, LANES), step_columns)
        sum_out[columns, :] = lax.dot_general(
            activated[:, columns], upstreams, (((0,), (0,)), ((), ())),
            preferred_element_type=jnp.float32,
        ).astype(jnp.bfloat16)
        if inside:
            scatter.give_core(1, part)
        return carry

    lax.fori_loop(0, parts, out_part, 0)
    for start in range(0, expand, CHUNK):
        columns = slice(start, start + CHUNK)
        sum_in[:, columns] = lax.dot_general(
            normed_low[...], hidden_grad[:, columns], (((0,), (0,)), ((), ())),
            preferred_element_type=jnp.float32,
        ).astype(jnp.bfloat16)
    if inside:
        for turn in range(parts):
            scatter.give_core(0, place.far_first(turn))
        for turn in range(parts):
            scatter.over_core(turn)

    kernel_acc[...] = jnp.zeros_like(kernel_acc)

    def tap_grads(flat, carry):
        micro = flat // lane_tiles
        lanes = lane_tile(flat % lane_tiles)
        values = tiles[micro, :, lanes].astype(jnp.float32)
        values = values.reshape(slots, SIDE, SIDE, LANES)
        grads = normed[rows_of(micro), lanes].reshape(slots, SIDE, SIDE, LANES)
        for across in range(TAPS):
            shifted = shift_columns(values, across - 3)
            for vertical in range(TAPS):
                offset = vertical - 3
                low, high = max(0, -offset), min(SIDE, SIDE - offset)
                product = shifted[:, low + offset : high + offset] * grads[:, low:high]
                kernel_acc[vertical * TAPS + across, :, lanes] += jnp.sum(product, axis=(0, 1))
        return carry

    lax.fori_loop(0, micro_count * lane_tiles, tap_grads, 0)
    small = stage.at[0] if inside else small_ref
    small[0:HEAD_ROW, :] = jnp.sum(kernel_acc[...], axis=1)

    @pl.when(is_last)
    def _():
        for step in range(1, section_count):
            head_copy(step).wait_send()

    @pl.when(jnp.logical_not(is_last))
    def _():
        head_copy(1).wait_recv()

    small[HEAD_ROW:SMALL_ROWS, :] = head_block[...]
    if inside:
        partners = (
            place.at(core=1 - place.core),
            place.at(across=1 - place.across),
            place.at(row=1 - place.row),
        )

        def small_copy(turn):
            return remote(
                stage.at[turn], landed.at[turn], small_send.at[turn], small_recv.at[turn],
                partners[turn],
            )

        def back_copy(step):
            return remote(
                stage.at[3], home_small, back_send.at[step - 1], back_recv,
                place.at(along=lax.rem(place.along + step, 4)),
            )

        small_copy(0).start()
        for turn in range(parts):
            scatter.over_plane(turn)
            if turn < 3:
                small_copy(turn).wait()
                stage[turn + 1] = stage[turn] + landed[turn]
                if turn < 2:
                    small_copy(turn + 1).start()
                else:

                    @pl.when(place.keeper)
                    def _():
                        for step in range(1, 4):
                            back_copy(step).start()
                        home_small[...] = stage[3]

        @pl.when(jnp.logical_not(place.keeper))
        def _():
            back_copy(1).wait_recv()

        small_ref[...] = home_small[...]
        scatter.finish((grad_in_ref, grad_out_ref))
        scatter.wait_sends()
        gather.wait_sends()

        @pl.when(place.keeper)
        def _():
            for step in range(1, 4):
                back_copy(step).wait_send()
                taps_copy(step).wait_send()

        @pl.when(is_source & (place.along != 0))
        def _():
            for micro in range(micro_count):
                crop_copy(micro).wait_send()

        @pl.when(is_source & (place.along != 3))
        def _():
            label_copy.wait_send()

    def finish(micro, carry):
        @pl.when(jnp.logical_not(is_last))
        def _():
            tile_copy(micro).wait_send()

        @pl.when(jnp.logical_not(is_first))
        def _():
            up_copy(micro).wait_send()

        return carry

    lax.fori_loop(0, micro_count, finish, 0)


def body(crop_maps, target_maps, crop_counts, depth_kernels, weight_in, weight_out, head_weight):
    section_count = lax.axis_size("section")
    micro_count, slots = crop_maps.shape[1:3]
    width = crop_maps.shape[-1]
    cells = slots * SIDE * SIDE
    expand = weight_in.shape[2]
    live = jnp.arange(slots)[None, :] < crop_counts[0][:, None]
    entering = crop_maps[0] * live[:, :, None, None, None].astype(jnp.bfloat16)
    entering = entering.reshape(micro_count, cells, width)
    targets = target_maps[0].reshape(micro_count, cells, 1).astype(jnp.float32)
    weights = jnp.broadcast_to(
        live[:, :, None].astype(jnp.float32), (micro_count, slots, SIDE * SIDE)
    ).reshape(micro_count, cells, 1)
    lane = jnp.arange(LANES)
    labels = jnp.where(lane == 0, targets, 0.0) + jnp.where(lane == 1, weights, 0.0)
    group_count = lax.axis_size("dp")
    height_in, height_out = weight_in.shape[1], weight_out.shape[1]
    inside = (
        section_count == 4
        and group_count == 8
        and height_in % 16 == 0
        and height_out % 16 == 0
        and 2 * height_out % LANES == 0
    )
    first, second = weight_in[0], weight_out[0]
    if not inside:
        first = lax.all_gather(first, "dp", axis=0, tiled=True)
        second = lax.all_gather(second, "dp", axis=0, tiled=True)
    low, full = jnp.bfloat16, jnp.float32
    every = micro_count * cells
    in_vmem = pl.BlockSpec(memory_space=pltpu.VMEM)
    shapes = [
        ((height_in, expand), full) if inside else ((width, expand), low),
        ((height_out, width), full) if inside else ((expand, width), low),
        ((SMALL_ROWS, width), full),
    ]
    scratch = [
        pltpu.VMEM((micro_count, cells, width), low),
        pltpu.VMEM((micro_count, cells, width), low),
        pltpu.VMEM((micro_count, cells, width), low),
        pltpu.VMEM((micro_count, cells, width), low),
        pltpu.VMEM((cells, width), full),
        pltpu.VMEM((every, width), full),
        pltpu.VMEM((every, width), low),
        pltpu.VMEM((every, LANES), full),
        pltpu.VMEM((every, expand), low),
        pltpu.VMEM((every, expand), full),
        pltpu.VMEM((every, expand), low),
        pltpu.VMEM((HEAD_ROW, SIDE, width), full),
        pltpu.VMEM((SMALL_ROWS - HEAD_ROW, width), full),
        pltpu.SemaphoreType.DMA((micro_count,)),
        pltpu.SemaphoreType.DMA((micro_count,)),
        pltpu.SemaphoreType.DMA((micro_count,)),
        pltpu.SemaphoreType.DMA((micro_count,)),
        pltpu.SemaphoreType.DMA((section_count - 1,)),
        pltpu.SemaphoreType.DMA,
    ]
    if inside:
        dma = pltpu.SemaphoreType.DMA
        whole = [pltpu.VMEM((width, expand), low), pltpu.VMEM((expand, width), low)]
        slabs = [
            pltpu.VMEM((4, height_in, expand), low), pltpu.VMEM((4, height_out, width), low)
        ]
        scratch += whole * 3 + slabs * 2
        scratch += [
            pltpu.VMEM((height_in, expand), low),
            pltpu.VMEM((height_out, width), low),
            pltpu.VMEM((4, SMALL_ROWS, width), full),
            pltpu.VMEM((3, SMALL_ROWS, width), full),
            pltpu.VMEM((SMALL_ROWS, width), full),
            pltpu.VMEM(depth_kernels.shape[1:], full),
            pltpu.VMEM(labels.shape, full),
            dma((2, 8)), dma((2,)), dma((8,)), dma((4,)), dma((4,)),
            dma((4,)), dma((4,)), dma((4,)), dma((4,)), dma((4,)), dma((4,)), dma((4,)), dma((2,)),
            dma((3,)), dma((3,)), dma((3,)), dma, dma((micro_count,)), dma, dma,
            dma((3,)), dma,
        ]
    grad_in, grad_out, small = pl.pallas_call(
        functools.partial(
            kernel, section_count, micro_count, slots, inside
        ),
        out_shape=tuple(jax.ShapeDtypeStruct(shape, kind) for shape, kind in shapes),
        in_specs=[in_vmem] * 6,
        out_specs=(in_vmem,) * 3,
        scratch_shapes=scratch,
        compiler_params=pltpu.CompilerParams(
            collective_id=0, has_side_effects=True, vmem_limit_bytes=60 * 1024 * 1024
        ),
        cost_estimate=pl.CostEstimate(
            flops=12 * every * width * expand, bytes_accessed=8 * width * expand, transcendentals=0
        ),
    )(entering, labels, depth_kernels[0], first, second, head_weight[None])
    if not inside:
        grad_in = lax.psum_scatter(grad_in, "dp", scatter_dimension=0, tiled=True).astype(full)
        grad_out = lax.psum_scatter(grad_out, "dp", scatter_dimension=0, tiled=True).astype(full)
        small = lax.psum(small, "dp")
    taps = depth_kernels.shape[1]
    return (
        grad_in[None],
        grad_out[None],
        small[:taps][None],
        small[HEAD_ROW],
        small[HEAD_ROW + 1, 0],
    )


def solution(mesh):
    return jax.shard_map(
        body,
        mesh=mesh,
        in_specs=(
            P("dp", None, None, None, None, None),
            P("dp", None, None, None, None),
            P("dp", None),
            P("section", None, None),
            P("section", "dp", None),
            P("section", "dp", None),
            P(),
        ),
        out_specs=(
            P("section", "dp", None),
            P("section", "dp", None),
            P("section", None, None),
            P(),
            P(),
        ),
        check_vma=False,
    )
```

```python
import functools

import jax
import jax.numpy as jnp
from jax import lax
from jax.experimental import pallas as pl
from jax.experimental.pallas import tpu as pltpu
from jax.sharding import PartitionSpec as P

EPSILON = 1e-06
SQRT_HALF = 0.7071067811865476
INV_ROOT_TWO_PI = 0.3989422804014327
MESH = pl.DeviceIdType.MESH
LANES = 128
CHUNK = 512
TAPS = 7
SIDE = 8
SMALL_ROWS = 64
HEAD_ROW = 56


def shift_columns(values, distance):
    if distance == 0:
        return values
    column = lax.broadcasted_iota(jnp.int32, values.shape, 2)
    moved = pltpu.roll(values, (-distance) % SIDE, 2)
    keep = (column + distance >= 0) & (column + distance < SIDE)
    return jnp.where(keep, moved, 0.0)


def valid_rows(offset):
    return range(max(0, -offset), min(SIDE, SIDE - offset))


def depthwise(values, taps_ref, lanes, flip):
    rows = [jnp.zeros_like(values[:, 0]) for _ in range(SIDE)]
    for across in range(TAPS):
        shifted = shift_columns(values, across - 3)
        for vertical in range(TAPS):
            tap = vertical * TAPS + across
            if flip:
                tap = TAPS * TAPS - 1 - tap
            weight = taps_ref[pl.ds(tap, 1), lanes].reshape(1, 1, LANES)
            for row in valid_rows(vertical - 3):
                rows[row] = rows[row] + shifted[:, row + vertical - 3] * weight
    return jnp.stack(rows, axis=1)


def lane_tile(index):
    return pl.ds(pl.multiple_of(index * LANES, LANES), LANES)


class Place:
    def __init__(self):
        group, self.home = lax.axis_index("dp"), lax.axis_index("section")
        self.group = group
        self.along, self.across = group // 2, lax.rem(group, 2)
        self.row, self.core = self.home // 2, lax.rem(self.home, 2)
        self.role = self.swap(self.along)
        self.role_row, self.role_core = lax.rem(self.along, 2), self.along // 2
        self.keeper = self.home == self.role
        self.lands = (self.row == self.role_row, self.row != self.role_row)

    def swap(self, index):
        return 2 * lax.rem(index, 2) + index // 2

    def at(self, along=None, across=None, row=None, core=None):
        along = self.along if along is None else along
        across = self.across if across is None else across
        row = self.row if row is None else row
        core = self.core if core is None else core
        return {"dp": 2 * along + across, "section": 2 * row + core}

    def near_first(self, turn):
        return jnp.where(
            self.along < 2, lax.rem(self.along + turn, 4), lax.rem(self.along - turn + 4, 4)
        )

    def far_first(self, turn):
        return jnp.where(self.along < 2, 3 - turn, turn)


def remote(source, target, send_sem, recv_sem, device):
    return pltpu.make_async_remote_copy(
        src_ref=source, dst_ref=target, send_sem=send_sem, recv_sem=recv_sem,
        device_id=device, device_id_type=MESH,
    )


def slab(ref, place, height):
    return ref.at[pl.ds(pl.multiple_of(place * height, 16), height), :]


class Gather:
    def __init__(self, place, weights, recv, first_send, core_send, across_send, row_send):
        self.place, self.weights, self.recv = place, weights, recv
        self.first_send, self.core_send = first_send, core_send
        self.across_send, self.row_send = across_send, row_send

    def shard(self, which, origin):
        own, full = self.weights[which]
        return slab(full, origin, own.shape[0])

    def launch(self, which):
        place = self.place
        plane = place.swap(place.home)
        target = self.shard(which, place.group)
        return remote(
            self.weights[which][0], target, self.first_send.at[which],
            self.recv.at[which, place.group],
            place.at(along=plane, core=which, row=place.row if which == 0 else 1 - place.row),
        )

    def stays(self, which):
        return self.place.keeper & (self.place.core == which) & self.place.lands[which]

    def spread(self, which, origin, sem, device):
        target = self.shard(which, origin)
        return remote(target, target, sem, self.recv.at[which, origin], device)

    def to_core(self, which, origin):
        place = self.place
        return self.spread(
            which, origin, self.core_send.at[origin], place.at(core=1 - place.core)
        )

    def to_across(self, which, along):
        place = self.place
        return self.spread(
            which, 2 * along + place.across, self.across_send.at[along],
            place.at(across=1 - place.across),
        )

    def to_row(self, which, along):
        place = self.place
        return self.spread(
            which, 2 * along + place.across, self.row_send.at[along], place.at(row=1 - place.row)
        )

    def start(self):
        for which in range(2):
            stays = self.stays(which)

            @pl.when(jnp.logical_not(stays))
            def _():
                self.launch(which).start()

            @pl.when(stays)
            def _():
                own, full = self.weights[which]
                height = own.shape[0]
                start = pl.multiple_of(self.place.group * height, 16)
                full[pl.ds(start, height), :] = own[...]

    def run(self):
        place = self.place
        for which in range(2):

            @pl.when(place.core == which)
            def _():
                for turn in range(4):
                    along = place.near_first(turn)
                    origin = 2 * along + place.across
                    if turn == 0:

                        @pl.when(jnp.logical_not(self.stays(which)))
                        def _():
                            self.to_core(which, origin).wait_recv()
                    else:
                        self.to_core(which, origin).wait_recv()
                    self.to_across(which, along).start()

                    @pl.when(place.lands[which])
                    def _():
                        self.to_row(which, along).start()

                    self.to_core(which, origin).start()
                for turn in range(4):
                    origin = 2 * place.near_first(turn) + 1 - place.across
                    self.to_core(which, origin).wait_recv()
                    self.to_core(which, origin).start()

        for which in range(2):

            @pl.when(place.core != which)
            def _():
                for origin in range(8):
                    self.to_core(which, origin).wait_recv()

    def wait_sends(self):
        place = self.place
        for which in range(2):

            @pl.when(jnp.logical_not(self.stays(which)))
            def _():
                self.launch(which).wait_send()

            @pl.when(place.core == which)
            def _():
                for along in range(4):
                    self.to_across(which, along).wait_send()

                    @pl.when(place.lands[which])
                    def _():
                        self.to_row(which, along).wait_send()

                for origin in range(8):
                    self.to_core(which, origin).wait_send()


class Scatter:
    def __init__(self, place, sums, cores, sides, rows, homes, sems):
        self.place, self.sums, self.cores = place, sums, cores
        self.sides, self.rows, self.homes = sides, rows, homes
        (
            self.core_send, self.core_recv, self.side_send, self.side_recv,
            self.row_send, self.row_recv, self.home_send, self.home_recv,
        ) = sems

    def height(self, which):
        return self.sides[which].shape[1]

    def core_copy(self, which, along):
        place, height = self.place, 2 * self.height(which)
        return remote(
            slab(self.sums[which], along, height), slab(self.cores[which], along, height),
            self.core_send.at[along], self.core_recv.at[along], place.at(core=1 - place.core),
        )

    def side_copy(self, which, along):
        place = self.place
        source = slab(self.sums[which], 2 * along + 1 - place.across, self.height(which))
        return remote(
            source, self.sides[which].at[along], self.side_send.at[along],
            self.side_recv.at[along], place.at(across=1 - place.across),
        )

    def row_copy(self, which, along):
        place = self.place
        source = slab(self.sums[which], 2 * along + place.across, self.height(which))
        return remote(
            source, self.rows[which].at[along], self.row_send.at[along],
            self.row_recv.at[along], place.at(row=1 - place.row),
        )

    def home_copy(self, which, along):
        place = self.place
        source = slab(self.sums[which], 2 * along + place.across, self.height(which))
        return remote(
            source, self.homes[which], self.home_send.at[along], self.home_recv.at[which],
            place.at(along=along, core=place.role_core, row=place.role_row),
        )

    def goes(self, along):
        place = self.place
        return (along != place.along) | jnp.logical_not(place.keeper)

    def add(self, which, along, count, first, buffer):
        height = count * self.height(which)
        start = pl.multiple_of(first * self.height(which), 16)
        rows = pl.ds(start, height)
        total = self.sums[which][rows, :].astype(jnp.float32) + buffer.astype(jnp.float32)
        self.sums[which][rows, :] = total.astype(jnp.bfloat16)

    def give_core(self, which, along):
        @pl.when(self.place.core != which)
        def _():
            self.core_copy(which, along).start()

    def over_core(self, turn):
        along = self.place.far_first(turn)
        for which in range(2):

            @pl.when(self.place.core == which)
            def _():
                self.core_copy(which, along).wait_recv()
                height = 2 * self.height(which)
                start = pl.multiple_of(along * height, 16)
                self.add(which, along, 2, 2 * along, self.cores[which][pl.ds(start, height), :])
                self.side_copy(which, along).start()

    def over_plane(self, turn):
        place = self.place
        along = place.far_first(turn)
        for which in range(2):
            in_row = place.lands[which]

            @pl.when(place.core == which)
            def _():
                self.side_copy(which, along).wait_recv()
                own = 2 * along + place.across
                self.add(which, along, 1, own, self.sides[which][along])

                @pl.when(jnp.logical_not(in_row))
                def _():
                    self.row_copy(which, along).start()

                @pl.when(in_row)
                def _():
                    self.row_copy(which, along).wait_recv()
                    self.add(which, along, 1, own, self.rows[which][along])

                    @pl.when(self.goes(along))
                    def _():
                        self.home_copy(which, along).start()

                    @pl.when(jnp.logical_not(self.goes(along)))
                    def _():
                        height = self.height(which)
                        start = pl.multiple_of(own * height, 16)
                        self.homes[which][...] = self.sums[which][pl.ds(start, height), :]

    def finish(self, outputs):
        place = self.place
        for which in range(2):
            here = place.keeper & (place.core == which) & place.lands[which]

            @pl.when(jnp.logical_not(here))
            def _():
                self.home_copy(which, 0).wait_recv()

            outputs[which][...] = self.homes[which][...].astype(jnp.float32)

    def wait_sends(self):
        place = self.place
        for which in range(2):
            in_row = place.lands[which]
            for along in range(4):

                @pl.when(place.core != which)
                def _():
                    self.core_copy(which, along).wait_send()

                @pl.when(place.core == which)
                def _():
                    self.side_copy(which, along).wait_send()

                    @pl.when(jnp.logical_not(in_row))
                    def _():
                        self.row_copy(which, along).wait_send()

                    @pl.when(in_row & self.goes(along))
                    def _():
                        self.home_copy(which, along).wait_send()


def kernel(
    section_count, micro_count, slots, inside,
    x_ref, own_labels, own_taps, own_first, own_second, head_ref,
    grad_in_ref, grad_out_ref, small_ref,
    tiles, results, ups, tile_grads, mixed, normed, normed_low, inverse, activated, slope,
    hidden_grad, kernel_acc, head_block,
    tile_send, tile_recv, up_send, up_recv, head_send, head_recv,
    *more,
):
    last = section_count - 1
    if inside:
        place = Place()
        section = place.role
        peers = [
            {"dp": 2 * lax.rem(place.along + along, 4) + place.across,
             "section": lax.rem(place.home + other, 4)}
            for along in range(4) for other in range(4) if along + other > 0
        ]
        peers += [place.at(across=1 - place.across)]
    else:
        section = lax.axis_index("section")
        peers = [
            {"section": lax.rem(section + step, section_count)} for step in range(1, section_count)
        ]
    cells = slots * SIDE * SIDE
    width = x_ref.shape[-1]
    expand = own_first.shape[1]
    lane_tiles = width // LANES
    is_first = section == 0
    is_last = section == last
    following = jnp.minimum(section + 1, last)
    previous = jnp.maximum(section - 1, 0)

    def worker(index):
        return place.at(along=place.swap(index)) if inside else {"section": index}

    barrier = pltpu.get_barrier_semaphore()
    for peer in peers:
        pl.semaphore_signal(barrier, inc=1, device_id=peer, device_id_type=MESH)
    pl.semaphore_wait(barrier, len(peers))

    if inside:
        (
            first_ref, second_ref, sum_in, sum_out, core_in, core_out, side_in, side_out,
            row_in, row_out, home_in, home_out, stage, landed, home_small, taps_ref, labels,
            gather_recv, launch_send, spread_core, spread_across, spread_row,
            core_send, core_recv, side_send, side_recv, row_send, row_recv, home_send, home_recv,
            small_send, small_recv, back_send, back_recv, crop_send, label_send, label_recv,
            taps_send, taps_recv,
        ) = more
        is_source = place.along == place.home

        def crop_copy(micro):
            return remote(
                x_ref.at[micro], tiles.at[micro], crop_send.at[micro], tile_recv.at[micro],
                place.at(along=0),
            )

        label_copy = remote(own_labels, labels, label_send, label_recv, place.at(along=3))

        def taps_copy(step):
            device = {"dp": place.group, "section": lax.rem(place.home + step, 4)}
            return remote(own_taps, taps_ref, taps_send.at[step - 1], taps_recv, device)

        gather = Gather(
            place, ((own_first, first_ref), (own_second, second_ref)),
            gather_recv, launch_send, spread_core, spread_across, spread_row,
        )
        gather.start()

        @pl.when(place.keeper)
        def _():
            for step in range(1, 4):
                taps_copy(step).start()
            taps_ref[...] = own_taps[...]

        @pl.when(is_source & (place.along != 0))
        def _():
            for micro in range(micro_count):
                crop_copy(micro).start()

        @pl.when(is_source & (place.along != 3))
        def _():
            label_copy.start()

        @pl.when(is_source & (place.along == 3))
        def _():
            labels[...] = own_labels[...]

        gather.run()

        @pl.when(jnp.logical_not(place.keeper))
        def _():
            taps_copy(1).wait_recv()

        @pl.when((place.along == 3) & jnp.logical_not(is_source))
        def _():
            label_copy.wait_recv()

        own_crops = is_first & (place.home == 0)
    else:
        first_ref, second_ref, sum_in, sum_out = own_first, own_second, grad_in_ref, grad_out_ref
        taps_ref, labels, own_crops = own_taps, own_labels, is_first

    def rows_of(micro):
        return pl.ds(pl.multiple_of(micro * cells, cells), cells)

    def tile_copy(micro):
        return pltpu.make_async_remote_copy(
            src_ref=results.at[micro], dst_ref=tiles.at[micro],
            send_sem=tile_send.at[micro], recv_sem=tile_recv.at[micro],
            device_id=worker(following), device_id_type=MESH,
        )

    def up_copy(micro):
        return pltpu.make_async_remote_copy(
            src_ref=tile_grads.at[micro], dst_ref=ups.at[micro],
            send_sem=up_send.at[micro], recv_sem=up_recv.at[micro],
            device_id=worker(previous), device_id_type=MESH,
        )

    def head_copy(step):
        peer = lax.rem(section + step, section_count)
        return pltpu.make_async_remote_copy(
            src_ref=head_block, dst_ref=head_block,
            send_sem=head_send.at[step - 1], recv_sem=head_recv,
            device_id=worker(peer), device_id_type=MESH,
        )

    @pl.when(is_last)
    def _():
        head_block[...] = jnp.zeros_like(head_block)

    def forward(micro, carry):
        @pl.when(own_crops)
        def _():
            tiles[micro] = x_ref[micro]

        @pl.when(jnp.logical_not(own_crops))
        def _():
            tile_copy(micro).wait_recv()

        def mix(index, carry):
            lanes = lane_tile(index)
            values = tiles[micro, :, lanes].astype(jnp.float32)
            values = values.reshape(slots, SIDE, SIDE, LANES)
            mixed[:, lanes] = depthwise(values, taps_ref, lanes, False).reshape(cells, LANES)
            return carry

        lax.fori_loop(0, lane_tiles, mix, 0)
        rows = rows_of(micro)
        value = mixed[...]
        centred = value - jnp.mean(value, axis=-1, keepdims=True)
        scale = lax.rsqrt(jnp.mean(centred * centred, axis=-1, keepdims=True) + EPSILON)
        unit = centred * scale
        low = unit.astype(jnp.bfloat16)
        normed[rows, :] = unit
        normed_low[rows, :] = low
        inverse[rows, :] = jnp.broadcast_to(scale, (cells, LANES))
        total = tiles[micro].astype(jnp.float32)
        for start in range(0, expand, CHUNK):
            columns = slice(start, start + CHUNK)
            hidden = jnp.dot(low, first_ref[:, columns], preferred_element_type=jnp.float32)
            portion = 0.5 * (1.0 + lax.erf(hidden * SQRT_HALF))
            active = (hidden * portion).astype(jnp.bfloat16)
            activated[rows, columns] = active
            slope[rows, columns] = (
                portion + hidden * jnp.exp(-0.5 * hidden * hidden) * INV_ROOT_TWO_PI
            )
            total = total + jnp.dot(
                active, second_ref[columns, :], preferred_element_type=jnp.float32
            )
        results[micro] = total.astype(jnp.bfloat16)

        @pl.when(jnp.logical_not(is_last))
        def _():
            tile_copy(micro).start()

        @pl.when(is_last)
        def _():
            final = results[micro].astype(jnp.float32)
            logits = jnp.sum(final * head_ref[...], axis=-1, keepdims=True)
            truth = labels[micro, :, 0:1]
            weight = labels[micro, :, 1:2]
            factor = 1.0 / (micro_count * slots)
            softplus = jnp.maximum(logits, 0.0) + jnp.log1p(jnp.exp(-jnp.abs(logits)))
            loss = jnp.sum(weight * (softplus - truth * logits)) * factor
            logit_grad = (1.0 / (1.0 + jnp.exp(-logits)) - truth) * weight * factor
            ups[micro] = (logit_grad * head_ref[...]).astype(jnp.bfloat16)
            term = jnp.sum(logit_grad * final, axis=0, keepdims=True)
            head_block[0:1, :] += term
            head_block[1:2, :] += jnp.full((1, width), loss)

        return carry

    lax.fori_loop(0, micro_count, forward, 0)

    @pl.when(is_last)
    def _():
        for step in range(1, section_count):
            head_copy(step).start()

    def backward(micro, carry):
        @pl.when(jnp.logical_not(is_last))
        def _():
            up_copy(micro).wait_recv()

        rows = rows_of(micro)
        upstream = ups[micro]
        total = jnp.zeros((cells, width), jnp.float32)
        for start in range(0, expand, CHUNK):
            columns = slice(start, start + CHUNK)
            through = lax.dot_general(
                upstream, second_ref[columns, :], (((1,), (1,)), ((), ())),
                preferred_element_type=jnp.float32,
            )
            grad = (through * slope[rows, columns]).astype(jnp.bfloat16)
            hidden_grad[rows, columns] = grad
            total = total + lax.dot_general(
                grad, first_ref[:, columns], (((1,), (1,)), ((), ())),
                preferred_element_type=jnp.float32,
            )
        unit = normed[rows, :]
        mixed_grad = inverse[rows, 0:1] * (
            total
            - jnp.mean(total, axis=-1, keepdims=True)
            - unit * jnp.mean(total * unit, axis=-1, keepdims=True)
        )
        normed[rows, :] = mixed_grad

        def unmix(index, carry):
            lanes = lane_tile(index)
            values = normed[rows, lanes].reshape(slots, SIDE, SIDE, LANES)
            back = depthwise(values, taps_ref, lanes, True).reshape(cells, LANES)
            back = back + ups[micro, :, lanes].astype(jnp.float32)
            tile_grads[micro, :, lanes] = back.astype(jnp.bfloat16)
            return carry

        @pl.when(jnp.logical_not(is_first))
        def _():
            lax.fori_loop(0, lane_tiles, unmix, 0)
            up_copy(micro).start()

        return carry

    lax.fori_loop(0, micro_count, backward, 0)

    upstreams = ups[...].reshape(micro_count * cells, width)
    parts = expand // LANES // lane_tiles
    if inside:
        parts = 4
        scatter = Scatter(
            place, (sum_in, sum_out), (core_in, core_out), (side_in, side_out),
            (row_in, row_out), (home_in, home_out),
            (
                core_send, core_recv, side_send, side_recv,
                row_send, row_recv, home_send, home_recv,
            ),
        )
    step_columns = expand // parts

    def out_part(turn, carry):
        part = place.far_first(turn) if inside else turn
        columns = pl.ds(pl.multiple_of(part * step_columns, LANES), step_columns)
        sum_out[columns, :] = lax.dot_general(
            activated[:, columns], upstreams, (((0,), (0,)), ((), ())),
            preferred_element_type=jnp.float32,
        ).astype(jnp.bfloat16)
        if inside:
            scatter.give_core(1, part)
        return carry

    lax.fori_loop(0, parts, out_part, 0)
    for start in range(0, expand, CHUNK):
        columns = slice(start, start + CHUNK)
        sum_in[:, columns] = lax.dot_general(
            normed_low[...], hidden_grad[:, columns], (((0,), (0,)), ((), ())),
            preferred_element_type=jnp.float32,
        ).astype(jnp.bfloat16)
    if inside:
        for turn in range(parts):
            scatter.give_core(0, place.far_first(turn))
        for turn in range(parts):
            scatter.over_core(turn)

    kernel_acc[...] = jnp.zeros_like(kernel_acc)

    def tap_grads(flat, carry):
        micro = flat // lane_tiles
        lanes = lane_tile(flat % lane_tiles)
        values = tiles[micro, :, lanes].astype(jnp.float32)
        values = values.reshape(slots, SIDE, SIDE, LANES)
        grads = normed[rows_of(micro), lanes].reshape(slots, SIDE, SIDE, LANES)
        for across in range(TAPS):
            shifted = shift_columns(values, across - 3)
            for vertical in range(TAPS):
                offset = vertical - 3
                low, high = max(0, -offset), min(SIDE, SIDE - offset)
                product = shifted[:, low + offset : high + offset] * grads[:, low:high]
                kernel_acc[vertical * TAPS + across, :, lanes] += jnp.sum(product, axis=(0, 1))
        return carry

    lax.fori_loop(0, micro_count * lane_tiles, tap_grads, 0)
    small = stage.at[0] if inside else small_ref
    small[0:HEAD_ROW, :] = jnp.sum(kernel_acc[...], axis=1)

    @pl.when(is_last)
    def _():
        for step in range(1, section_count):
            head_copy(step).wait_send()

    @pl.when(jnp.logical_not(is_last))
    def _():
        head_copy(1).wait_recv()

    small[HEAD_ROW:SMALL_ROWS, :] = head_block[...]
    if inside:
        partners = (
            place.at(core=1 - place.core),
            place.at(across=1 - place.across),
            place.at(row=1 - place.row),
        )

        def small_copy(turn):
            return remote(
                stage.at[turn], landed.at[turn], small_send.at[turn], small_recv.at[turn],
                partners[turn],
            )

        def back_copy(step):
            return remote(
                stage.at[3], home_small, back_send.at[step - 1], back_recv,
                place.at(along=lax.rem(place.along + step, 4)),
            )

        small_copy(0).start()
        for turn in range(parts):
            scatter.over_plane(turn)
            if turn < 3:
                small_copy(turn).wait()
                stage[turn + 1] = stage[turn] + landed[turn]
                if turn < 2:
                    small_copy(turn + 1).start()
                else:

                    @pl.when(place.keeper)
                    def _():
                        for step in range(1, 4):
                            back_copy(step).start()
                        home_small[...] = stage[3]

        @pl.when(jnp.logical_not(place.keeper))
        def _():
            back_copy(1).wait_recv()

        small_ref[...] = home_small[...]
        scatter.finish((grad_in_ref, grad_out_ref))
        scatter.wait_sends()
        gather.wait_sends()

        @pl.when(place.keeper)
        def _():
            for step in range(1, 4):
                back_copy(step).wait_send()
                taps_copy(step).wait_send()

        @pl.when(is_source & (place.along != 0))
        def _():
            for micro in range(micro_count):
                crop_copy(micro).wait_send()

        @pl.when(is_source & (place.along != 3))
        def _():
            label_copy.wait_send()

    def finish(micro, carry):
        @pl.when(jnp.logical_not(is_last))
        def _():
            tile_copy(micro).wait_send()

        @pl.when(jnp.logical_not(is_first))
        def _():
            up_copy(micro).wait_send()

        return carry

    lax.fori_loop(0, micro_count, finish, 0)


def body(crop_maps, target_maps, crop_counts, depth_kernels, weight_in, weight_out, head_weight):
    section_count = lax.axis_size("section")
    micro_count, slots = crop_maps.shape[1:3]
    width = crop_maps.shape[-1]
    cells = slots * SIDE * SIDE
    expand = weight_in.shape[2]
    live = jnp.arange(slots)[None, :] < crop_counts[0][:, None]
    entering = crop_maps[0] * live[:, :, None, None, None].astype(jnp.bfloat16)
    entering = entering.reshape(micro_count, cells, width)
    targets = target_maps[0].reshape(micro_count, cells, 1).astype(jnp.float32)
    weights = jnp.broadcast_to(
        live[:, :, None].astype(jnp.float32), (micro_count, slots, SIDE * SIDE)
    ).reshape(micro_count, cells, 1)
    lane = jnp.arange(LANES)
    labels = jnp.where(lane == 0, targets, 0.0) + jnp.where(lane == 1, weights, 0.0)
    group_count = lax.axis_size("dp")
    height_in, height_out = weight_in.shape[1], weight_out.shape[1]
    inside = (
        section_count == 4
        and group_count == 8
        and height_in % 16 == 0
        and height_out % 16 == 0
        and 2 * height_out % LANES == 0
    )
    first, second = weight_in[0], weight_out[0]
    if not inside:
        first = lax.all_gather(first, "dp", axis=0, tiled=True)
        second = lax.all_gather(second, "dp", axis=0, tiled=True)
    low, full = jnp.bfloat16, jnp.float32
    every = micro_count * cells
    in_vmem = pl.BlockSpec(memory_space=pltpu.VMEM)
    shapes = [
        ((height_in, expand), full) if inside else ((width, expand), low),
        ((height_out, width), full) if inside else ((expand, width), low),
        ((SMALL_ROWS, width), full),
    ]
    scratch = [
        pltpu.VMEM((micro_count, cells, width), low),
        pltpu.VMEM((micro_count, cells, width), low),
        pltpu.VMEM((micro_count, cells, width), low),
        pltpu.VMEM((micro_count, cells, width), low),
        pltpu.VMEM((cells, width), full),
        pltpu.VMEM((every, width), full),
        pltpu.VMEM((every, width), low),
        pltpu.VMEM((every, LANES), full),
        pltpu.VMEM((every, expand), low),
        pltpu.VMEM((every, expand), full),
        pltpu.VMEM((every, expand), low),
        pltpu.VMEM((HEAD_ROW, SIDE, width), full),
        pltpu.VMEM((SMALL_ROWS - HEAD_ROW, width), full),
        pltpu.SemaphoreType.DMA((micro_count,)),
        pltpu.SemaphoreType.DMA((micro_count,)),
        pltpu.SemaphoreType.DMA((micro_count,)),
        pltpu.SemaphoreType.DMA((micro_count,)),
        pltpu.SemaphoreType.DMA((section_count - 1,)),
        pltpu.SemaphoreType.DMA,
    ]
    if inside:
        dma = pltpu.SemaphoreType.DMA
        whole = [pltpu.VMEM((width, expand), low), pltpu.VMEM((expand, width), low)]
        slabs = [
            pltpu.VMEM((4, height_in, expand), low), pltpu.VMEM((4, height_out, width), low)
        ]
        scratch += whole * 3 + slabs * 2
        scratch += [
            pltpu.VMEM((height_in, expand), low),
            pltpu.VMEM((height_out, width), low),
            pltpu.VMEM((4, SMALL_ROWS, width), full),
            pltpu.VMEM((3, SMALL_ROWS, width), full),
            pltpu.VMEM((SMALL_ROWS, width), full),
            pltpu.VMEM(depth_kernels.shape[1:], full),
            pltpu.VMEM(labels.shape, full),
            dma((2, 8)), dma((2,)), dma((8,)), dma((4,)), dma((4,)),
            dma((4,)), dma((4,)), dma((4,)), dma((4,)), dma((4,)), dma((4,)), dma((4,)), dma((2,)),
            dma((3,)), dma((3,)), dma((3,)), dma, dma((micro_count,)), dma, dma,
            dma((3,)), dma,
        ]
    grad_in, grad_out, small = pl.pallas_call(
        functools.partial(
            kernel, section_count, micro_count, slots, inside
        ),
        out_shape=tuple(jax.ShapeDtypeStruct(shape, kind) for shape, kind in shapes),
        in_specs=[in_vmem] * 6,
        out_specs=(in_vmem,) * 3,
        scratch_shapes=scratch,
        compiler_params=pltpu.CompilerParams(
            collective_id=0, has_side_effects=True, vmem_limit_bytes=60 * 1024 * 1024
        ),
        cost_estimate=pl.CostEstimate(
            flops=12 * every * width * expand, bytes_accessed=8 * width * expand, transcendentals=0
        ),
    )(entering, labels, depth_kernels[0], first, second, head_weight[None])
    if not inside:
        grad_in = lax.psum_scatter(grad_in, "dp", scatter_dimension=0, tiled=True).astype(full)
        grad_out = lax.psum_scatter(grad_out, "dp", scatter_dimension=0, tiled=True).astype(full)
        small = lax.psum(small, "dp")
    taps = depth_kernels.shape[1]
    return (
        grad_in[None],
        grad_out[None],
        small[:taps][None],
        small[HEAD_ROW],
        small[HEAD_ROW + 1, 0],
    )


def solution(mesh):
    return jax.shard_map(
        body,
        mesh=mesh,
        in_specs=(
            P("dp", None, None, None, None, None),
            P("dp", None, None, None, None),
            P("dp", None),
            P("section", None, None),
            P("section", "dp", None),
            P("section", "dp", None),
            P(),
        ),
        out_specs=(
            P("section", "dp", None),
            P("section", "dp", None),
            P("section", None, None),
            P(),
            P(),
        ),
        check_vma=False,
    )
```

```python
import functools

import jax
import jax.numpy as jnp
from jax import lax
from jax.experimental import pallas as pl
from jax.experimental.pallas import tpu as pltpu
from jax.sharding import PartitionSpec as P

EPSILON = 1e-06
SQRT_HALF = 0.7071067811865476
INV_ROOT_TWO_PI = 0.3989422804014327
MESH = pl.DeviceIdType.MESH
LANES = 128
CHUNK = 512
TAPS = 7
SIDE = 8
SMALL_ROWS = 64
HEAD_ROW = 56


def shift_columns(values, distance):
    if distance == 0:
        return values
    column = lax.broadcasted_iota(jnp.int32, values.shape, 2)
    moved = pltpu.roll(values, (-distance) % SIDE, 2)
    keep = (column + distance >= 0) & (column + distance < SIDE)
    return jnp.where(keep, moved, 0.0)


def valid_rows(offset):
    return range(max(0, -offset), min(SIDE, SIDE - offset))


def depthwise(values, taps_ref, lanes, flip):
    rows = [jnp.zeros_like(values[:, 0]) for _ in range(SIDE)]
    for across in range(TAPS):
        shifted = shift_columns(values, across - 3)
        for vertical in range(TAPS):
            tap = vertical * TAPS + across
            if flip:
                tap = TAPS * TAPS - 1 - tap
            weight = taps_ref[pl.ds(tap, 1), lanes].reshape(1, 1, LANES)
            for row in valid_rows(vertical - 3):
                rows[row] = rows[row] + shifted[:, row + vertical - 3] * weight
    return jnp.stack(rows, axis=1)


def lane_tile(index):
    return pl.ds(pl.multiple_of(index * LANES, LANES), LANES)


class Place:
    def __init__(self):
        group, self.home = lax.axis_index("dp"), lax.axis_index("section")
        self.group = group
        self.along, self.across = group // 2, lax.rem(group, 2)
        self.row, self.core = self.home // 2, lax.rem(self.home, 2)
        self.role = self.swap(self.along)
        self.role_row, self.role_core = lax.rem(self.along, 2), self.along // 2
        self.keeper = self.home == self.role
        self.lands = (self.row == self.role_row, self.row != self.role_row)

    def swap(self, index):
        return 2 * lax.rem(index, 2) + index // 2

    def at(self, along=None, across=None, row=None, core=None):
        along = self.along if along is None else along
        across = self.across if across is None else across
        row = self.row if row is None else row
        core = self.core if core is None else core
        return {"dp": 2 * along + across, "section": 2 * row + core}

    def near_first(self, turn):
        return jnp.where(
            self.along < 2, lax.rem(self.along + turn, 4), lax.rem(self.along - turn + 4, 4)
        )

    def far_first(self, turn):
        return jnp.where(self.along < 2, 3 - turn, turn)


def remote(source, target, send_sem, recv_sem, device):
    return pltpu.make_async_remote_copy(
        src_ref=source, dst_ref=target, send_sem=send_sem, recv_sem=recv_sem,
        device_id=device, device_id_type=MESH,
    )


def slab(ref, place, height):
    return ref.at[pl.ds(pl.multiple_of(place * height, 16), height), :]


class Gather:
    def __init__(self, place, weights, recv, first_send, core_send, across_send, row_send):
        self.place, self.weights, self.recv = place, weights, recv
        self.first_send, self.core_send = first_send, core_send
        self.across_send, self.row_send = across_send, row_send

    def shard(self, which, origin):
        own, full = self.weights[which]
        return slab(full, origin, own.shape[0])

    def launch(self, which):
        place = self.place
        plane = place.swap(place.home)
        target = self.shard(which, place.group)
        return remote(
            self.weights[which][0], target, self.first_send.at[which],
            self.recv.at[which, place.group],
            place.at(along=plane, core=which, row=place.row if which == 0 else 1 - place.row),
        )

    def stays(self, which):
        return self.place.keeper & (self.place.core == which) & self.place.lands[which]

    def spread(self, which, origin, sem, device):
        target = self.shard(which, origin)
        return remote(target, target, sem, self.recv.at[which, origin], device)

    def to_core(self, which, origin):
        place = self.place
        return self.spread(
            which, origin, self.core_send.at[origin], place.at(core=1 - place.core)
        )

    def to_across(self, which, along):
        place = self.place
        return self.spread(
            which, 2 * along + place.across, self.across_send.at[along],
            place.at(across=1 - place.across),
        )

    def to_row(self, which, origin):
        place = self.place
        return self.spread(
            which, origin, self.row_send.at[origin], place.at(row=1 - place.row)
        )

    def start(self):
        for which in range(2):
            stays = self.stays(which)

            @pl.when(jnp.logical_not(stays))
            def _():
                self.launch(which).start()

            @pl.when(stays)
            def _():
                own, full = self.weights[which]
                height = own.shape[0]
                start = pl.multiple_of(self.place.group * height, 16)
                full[pl.ds(start, height), :] = own[...]

    def run(self):
        place = self.place
        for which in range(2):

            @pl.when(place.core == which)
            def _():
                for turn in range(4):
                    along = place.near_first(turn)
                    origin = 2 * along + place.across
                    if turn == 0:

                        @pl.when(jnp.logical_not(self.stays(which)))
                        def _():
                            self.to_core(which, origin).wait_recv()
                    else:
                        self.to_core(which, origin).wait_recv()
                    if turn < 2:
                        self.to_across(which, along).start()

                    @pl.when(place.lands[which])
                    def _():
                        if turn >= 2:
                            self.to_across(which, along).start()
                        self.to_row(which, origin).start()

                    self.to_core(which, origin).start()
                for turn in range(4):
                    origin = 2 * place.near_first(turn) + 1 - place.across
                    self.to_core(which, origin).wait_recv()
                    if turn >= 2:

                        @pl.when(place.lands[which])
                        def _():
                            self.to_row(which, origin).start()

                    self.to_core(which, origin).start()

        for which in range(2):

            @pl.when(place.core != which)
            def _():
                for origin in range(8):
                    self.to_core(which, origin).wait_recv()

    def wait_sends(self):
        place = self.place
        for which in range(2):

            @pl.when(jnp.logical_not(self.stays(which)))
            def _():
                self.launch(which).wait_send()

            @pl.when(place.core == which)
            def _():
                for turn in range(4):
                    along = place.near_first(turn)
                    if turn < 2:
                        self.to_across(which, along).wait_send()

                    @pl.when(place.lands[which])
                    def _():
                        self.to_row(which, 2 * along + place.across).wait_send()
                        if turn >= 2:
                            self.to_across(which, along).wait_send()
                            self.to_row(which, 2 * along + 1 - place.across).wait_send()

                for origin in range(8):
                    self.to_core(which, origin).wait_send()


class Scatter:
    def __init__(self, place, sums, cores, sides, rows, homes, sems):
        self.place, self.sums, self.cores = place, sums, cores
        self.sides, self.rows, self.homes = sides, rows, homes
        (
            self.core_send, self.core_recv, self.side_send, self.side_recv,
            self.row_send, self.row_recv, self.home_send, self.home_recv,
        ) = sems

    def height(self, which):
        return self.sides[which].shape[1]

    def core_copy(self, which, along):
        place, height = self.place, 2 * self.height(which)
        return remote(
            slab(self.sums[which], along, height), slab(self.cores[which], along, height),
            self.core_send.at[along], self.core_recv.at[along], place.at(core=1 - place.core),
        )

    def side_copy(self, which, along):
        place = self.place
        source = slab(self.sums[which], 2 * along + 1 - place.across, self.height(which))
        return remote(
            source, self.sides[which].at[along], self.side_send.at[along],
            self.side_recv.at[along], place.at(across=1 - place.across),
        )

    def row_copy(self, which, along):
        place = self.place
        source = slab(self.sums[which], 2 * along + place.across, self.height(which))
        return remote(
            source, self.rows[which].at[along], self.row_send.at[along],
            self.row_recv.at[along], place.at(row=1 - place.row),
        )

    def home_copy(self, which, along):
        place = self.place
        source = slab(self.sums[which], 2 * along + place.across, self.height(which))
        return remote(
            source, self.homes[which], self.home_send.at[along], self.home_recv.at[which],
            place.at(along=along, core=place.role_core, row=place.role_row),
        )

    def goes(self, along):
        place = self.place
        return (along != place.along) | jnp.logical_not(place.keeper)

    def add(self, which, along, count, first, buffer):
        height = count * self.height(which)
        start = pl.multiple_of(first * self.height(which), 16)
        rows = pl.ds(start, height)
        total = self.sums[which][rows, :].astype(jnp.float32) + buffer.astype(jnp.float32)
        self.sums[which][rows, :] = total.astype(jnp.bfloat16)

    def give_core(self, which, along):
        @pl.when(self.place.core != which)
        def _():
            self.core_copy(which, along).start()

    def over_core(self, turn):
        along = self.place.far_first(turn)
        for which in range(2):

            @pl.when(self.place.core == which)
            def _():
                self.core_copy(which, along).wait_recv()
                height = 2 * self.height(which)
                start = pl.multiple_of(along * height, 16)
                self.add(which, along, 2, 2 * along, self.cores[which][pl.ds(start, height), :])
                self.side_copy(which, along).start()

    def over_plane(self, turn):
        place = self.place
        along = place.far_first(turn)
        for which in range(2):
            in_row = place.lands[which]

            @pl.when(place.core == which)
            def _():
                self.side_copy(which, along).wait_recv()
                own = 2 * along + place.across
                self.add(which, along, 1, own, self.sides[which][along])

                @pl.when(jnp.logical_not(in_row))
                def _():
                    self.row_copy(which, along).start()

                @pl.when(in_row)
                def _():
                    self.row_copy(which, along).wait_recv()
                    self.add(which, along, 1, own, self.rows[which][along])

                    @pl.when(self.goes(along))
                    def _():
                        self.home_copy(which, along).start()

                    @pl.when(jnp.logical_not(self.goes(along)))
                    def _():
                        height = self.height(which)
                        start = pl.multiple_of(own * height, 16)
                        self.homes[which][...] = self.sums[which][pl.ds(start, height), :]

    def finish(self, outputs):
        place = self.place
        for which in range(2):
            here = place.keeper & (place.core == which) & place.lands[which]

            @pl.when(jnp.logical_not(here))
            def _():
                self.home_copy(which, 0).wait_recv()

            outputs[which][...] = self.homes[which][...].astype(jnp.float32)

    def wait_sends(self):
        place = self.place
        for which in range(2):
            in_row = place.lands[which]
            for along in range(4):

                @pl.when(place.core != which)
                def _():
                    self.core_copy(which, along).wait_send()

                @pl.when(place.core == which)
                def _():
                    self.side_copy(which, along).wait_send()

                    @pl.when(jnp.logical_not(in_row))
                    def _():
                        self.row_copy(which, along).wait_send()

                    @pl.when(in_row & self.goes(along))
                    def _():
                        self.home_copy(which, along).wait_send()


def kernel(
    section_count, micro_count, slots, inside,
    x_ref, own_labels, own_taps, own_first, own_second, head_ref,
    grad_in_ref, grad_out_ref, small_ref,
    tiles, results, ups, tile_grads, mixed, normed, normed_low, inverse, activated, slope,
    hidden_grad, kernel_acc, head_block,
    tile_send, tile_recv, up_send, up_recv, head_send, head_recv,
    *more,
):
    last = section_count - 1
    if inside:
        place = Place()
        section = place.role
        peers = [
            {"dp": 2 * lax.rem(place.along + along, 4) + place.across,
             "section": lax.rem(place.home + other, 4)}
            for along in range(4) for other in range(4) if along + other > 0
        ]
        peers += [place.at(across=1 - place.across)]
    else:
        section = lax.axis_index("section")
        peers = [
            {"section": lax.rem(section + step, section_count)} for step in range(1, section_count)
        ]
    cells = slots * SIDE * SIDE
    width = x_ref.shape[-1]
    expand = own_first.shape[1]
    lane_tiles = width // LANES
    is_first = section == 0
    is_last = section == last
    following = jnp.minimum(section + 1, last)
    previous = jnp.maximum(section - 1, 0)

    def worker(index):
        return place.at(along=place.swap(index)) if inside else {"section": index}

    barrier = pltpu.get_barrier_semaphore()
    for peer in peers:
        pl.semaphore_signal(barrier, inc=1, device_id=peer, device_id_type=MESH)
    pl.semaphore_wait(barrier, len(peers))

    if inside:
        (
            first_ref, second_ref, sum_in, sum_out, core_in, core_out, side_in, side_out,
            row_in, row_out, home_in, home_out, stage, landed, home_small, taps_ref, labels,
            gather_recv, launch_send, spread_core, spread_across, spread_row,
            core_send, core_recv, side_send, side_recv, row_send, row_recv, home_send, home_recv,
            small_send, small_recv, back_send, back_recv, crop_send, label_send, label_recv,
            taps_send, taps_recv,
        ) = more
        is_source = place.along == place.home

        def crop_copy(micro):
            return remote(
                x_ref.at[micro], tiles.at[micro], crop_send.at[micro], tile_recv.at[micro],
                place.at(along=0),
            )

        label_copy = remote(own_labels, labels, label_send, label_recv, place.at(along=3))

        def taps_copy(step):
            device = {"dp": place.group, "section": lax.rem(place.home + step, 4)}
            return remote(own_taps, taps_ref, taps_send.at[step - 1], taps_recv, device)

        gather = Gather(
            place, ((own_first, first_ref), (own_second, second_ref)),
            gather_recv, launch_send, spread_core, spread_across, spread_row,
        )
        gather.start()

        @pl.when(place.keeper)
        def _():
            for step in range(1, 4):
                taps_copy(step).start()
            taps_ref[...] = own_taps[...]

        @pl.when(is_source & (place.along != 0))
        def _():
            for micro in range(micro_count):
                crop_copy(micro).start()

        @pl.when(is_source & (place.along != 3))
        def _():
            label_copy.start()

        @pl.when(is_source & (place.along == 3))
        def _():
            labels[...] = own_labels[...]

        gather.run()

        @pl.when(jnp.logical_not(place.keeper))
        def _():
            taps_copy(1).wait_recv()

        @pl.when((place.along == 3) & jnp.logical_not(is_source))
        def _():
            label_copy.wait_recv()

        own_crops = is_first & (place.home == 0)
    else:
        first_ref, second_ref, sum_in, sum_out = own_first, own_second, grad_in_ref, grad_out_ref
        taps_ref, labels, own_crops = own_taps, own_labels, is_first

    def rows_of(micro):
        return pl.ds(pl.multiple_of(micro * cells, cells), cells)

    def tile_copy(micro):
        return pltpu.make_async_remote_copy(
            src_ref=results.at[micro], dst_ref=tiles.at[micro],
            send_sem=tile_send.at[micro], recv_sem=tile_recv.at[micro],
            device_id=worker(following), device_id_type=MESH,
        )

    def up_copy(micro):
        return pltpu.make_async_remote_copy(
            src_ref=tile_grads.at[micro], dst_ref=ups.at[micro],
            send_sem=up_send.at[micro], recv_sem=up_recv.at[micro],
            device_id=worker(previous), device_id_type=MESH,
        )

    def head_copy(step):
        peer = lax.rem(section + step, section_count)
        return pltpu.make_async_remote_copy(
            src_ref=head_block, dst_ref=head_block,
            send_sem=head_send.at[step - 1], recv_sem=head_recv,
            device_id=worker(peer), device_id_type=MESH,
        )

    @pl.when(is_last)
    def _():
        head_block[...] = jnp.zeros_like(head_block)

    def forward(micro, carry):
        @pl.when(own_crops)
        def _():
            tiles[micro] = x_ref[micro]

        @pl.when(jnp.logical_not(own_crops))
        def _():
            tile_copy(micro).wait_recv()

        def mix(index, carry):
            lanes = lane_tile(index)
            values = tiles[micro, :, lanes].astype(jnp.float32)
            values = values.reshape(slots, SIDE, SIDE, LANES)
            mixed[:, lanes] = depthwise(values, taps_ref, lanes, False).reshape(cells, LANES)
            return carry

        lax.fori_loop(0, lane_tiles, mix, 0)
        rows = rows_of(micro)
        value = mixed[...]
        centred = value - jnp.mean(value, axis=-1, keepdims=True)
        scale = lax.rsqrt(jnp.mean(centred * centred, axis=-1, keepdims=True) + EPSILON)
        unit = centred * scale
        low = unit.astype(jnp.bfloat16)
        normed[rows, :] = unit
        normed_low[rows, :] = low
        inverse[rows, :] = jnp.broadcast_to(scale, (cells, LANES))
        total = tiles[micro].astype(jnp.float32)
        for start in range(0, expand, CHUNK):
            columns = slice(start, start + CHUNK)
            hidden = jnp.dot(low, first_ref[:, columns], preferred_element_type=jnp.float32)
            portion = 0.5 * (1.0 + lax.erf(hidden * SQRT_HALF))
            active = (hidden * portion).astype(jnp.bfloat16)
            activated[rows, columns] = active
            slope[rows, columns] = (
                portion + hidden * jnp.exp(-0.5 * hidden * hidden) * INV_ROOT_TWO_PI
            )
            total = total + jnp.dot(
                active, second_ref[columns, :], preferred_element_type=jnp.float32
            )
        results[micro] = total.astype(jnp.bfloat16)

        @pl.when(jnp.logical_not(is_last))
        def _():
            tile_copy(micro).start()

        @pl.when(is_last)
        def _():
            final = results[micro].astype(jnp.float32)
            logits = jnp.sum(final * head_ref[...], axis=-1, keepdims=True)
            truth = labels[micro, :, 0:1]
            weight = labels[micro, :, 1:2]
            factor = 1.0 / (micro_count * slots)
            softplus = jnp.maximum(logits, 0.0) + jnp.log1p(jnp.exp(-jnp.abs(logits)))
            loss = jnp.sum(weight * (softplus - truth * logits)) * factor
            logit_grad = (1.0 / (1.0 + jnp.exp(-logits)) - truth) * weight * factor
            ups[micro] = (logit_grad * head_ref[...]).astype(jnp.bfloat16)
            term = jnp.sum(logit_grad * final, axis=0, keepdims=True)
            head_block[0:1, :] += term
            head_block[1:2, :] += jnp.full((1, width), loss)

        return carry

    lax.fori_loop(0, micro_count, forward, 0)

    @pl.when(is_last)
    def _():
        for step in range(1, section_count):
            head_copy(step).start()

    def backward(micro, carry):
        @pl.when(jnp.logical_not(is_last))
        def _():
            up_copy(micro).wait_recv()

        rows = rows_of(micro)
        upstream = ups[micro]
        total = jnp.zeros((cells, width), jnp.float32)
        for start in range(0, expand, CHUNK):
            columns = slice(start, start + CHUNK)
            through = lax.dot_general(
                upstream, second_ref[columns, :], (((1,), (1,)), ((), ())),
                preferred_element_type=jnp.float32,
            )
            grad = (through * slope[rows, columns]).astype(jnp.bfloat16)
            hidden_grad[rows, columns] = grad
            total = total + lax.dot_general(
                grad, first_ref[:, columns], (((1,), (1,)), ((), ())),
                preferred_element_type=jnp.float32,
            )
        unit = normed[rows, :]
        mixed_grad = inverse[rows, 0:1] * (
            total
            - jnp.mean(total, axis=-1, keepdims=True)
            - unit * jnp.mean(total * unit, axis=-1, keepdims=True)
        )
        normed[rows, :] = mixed_grad

        def unmix(index, carry):
            lanes = lane_tile(index)
            values = normed[rows, lanes].reshape(slots, SIDE, SIDE, LANES)
            back = depthwise(values, taps_ref, lanes, True).reshape(cells, LANES)
            back = back + ups[micro, :, lanes].astype(jnp.float32)
            tile_grads[micro, :, lanes] = back.astype(jnp.bfloat16)
            return carry

        @pl.when(jnp.logical_not(is_first))
        def _():
            lax.fori_loop(0, lane_tiles, unmix, 0)
            up_copy(micro).start()

        return carry

    lax.fori_loop(0, micro_count, backward, 0)

    upstreams = ups[...].reshape(micro_count * cells, width)
    parts = expand // LANES // lane_tiles
    if inside:
        parts = 4
        scatter = Scatter(
            place, (sum_in, sum_out), (core_in, core_out), (side_in, side_out),
            (row_in, row_out), (home_in, home_out),
            (
                core_send, core_recv, side_send, side_recv,
                row_send, row_recv, home_send, home_recv,
            ),
        )
    step_columns = expand // parts

    def out_part(turn, carry):
        part = place.far_first(turn) if inside else turn
        columns = pl.ds(pl.multiple_of(part * step_columns, LANES), step_columns)
        sum_out[columns, :] = lax.dot_general(
            activated[:, columns], upstreams, (((0,), (0,)), ((), ())),
            preferred_element_type=jnp.float32,
        ).astype(jnp.bfloat16)
        if inside:
            scatter.give_core(1, part)
        return carry

    lax.fori_loop(0, parts, out_part, 0)
    for start in range(0, expand, CHUNK):
        columns = slice(start, start + CHUNK)
        sum_in[:, columns] = lax.dot_general(
            normed_low[...], hidden_grad[:, columns], (((0,), (0,)), ((), ())),
            preferred_element_type=jnp.float32,
        ).astype(jnp.bfloat16)
    if inside:
        for turn in range(parts):
            scatter.give_core(0, place.far_first(turn))
        for turn in range(parts):
            scatter.over_core(turn)

    kernel_acc[...] = jnp.zeros_like(kernel_acc)

    def tap_grads(flat, carry):
        micro = flat // lane_tiles
        lanes = lane_tile(flat % lane_tiles)
        values = tiles[micro, :, lanes].astype(jnp.float32)
        values = values.reshape(slots, SIDE, SIDE, LANES)
        grads = normed[rows_of(micro), lanes].reshape(slots, SIDE, SIDE, LANES)
        for across in range(TAPS):
            shifted = shift_columns(values, across - 3)
            for vertical in range(TAPS):
                offset = vertical - 3
                low, high = max(0, -offset), min(SIDE, SIDE - offset)
                product = shifted[:, low + offset : high + offset] * grads[:, low:high]
                kernel_acc[vertical * TAPS + across, :, lanes] += jnp.sum(product, axis=(0, 1))
        return carry

    lax.fori_loop(0, micro_count * lane_tiles, tap_grads, 0)
    small = stage.at[0] if inside else small_ref
    small[0:HEAD_ROW, :] = jnp.sum(kernel_acc[...], axis=1)

    @pl.when(is_last)
    def _():
        for step in range(1, section_count):
            head_copy(step).wait_send()

    @pl.when(jnp.logical_not(is_last))
    def _():
        head_copy(1).wait_recv()

    small[HEAD_ROW:SMALL_ROWS, :] = head_block[...]
    if inside:
        partners = (
            place.at(core=1 - place.core),
            place.at(across=1 - place.across),
            place.at(row=1 - place.row),
        )

        def small_copy(turn):
            return remote(
                stage.at[turn], landed.at[turn], small_send.at[turn], small_recv.at[turn],
                partners[turn],
            )

        def back_copy(step):
            return remote(
                stage.at[3], home_small, back_send.at[step - 1], back_recv,
                place.at(along=lax.rem(place.along + step, 4)),
            )

        small_copy(0).start()
        for turn in range(parts):
            scatter.over_plane(turn)
            if turn < 3:
                small_copy(turn).wait()
                stage[turn + 1] = stage[turn] + landed[turn]
                if turn < 2:
                    small_copy(turn + 1).start()
                else:

                    @pl.when(place.keeper)
                    def _():
                        for step in range(1, 4):
                            back_copy(step).start()
                        home_small[...] = stage[3]

        @pl.when(jnp.logical_not(place.keeper))
        def _():
            back_copy(1).wait_recv()

        small_ref[...] = home_small[...]
        scatter.finish((grad_in_ref, grad_out_ref))
        scatter.wait_sends()
        gather.wait_sends()

        @pl.when(place.keeper)
        def _():
            for step in range(1, 4):
                back_copy(step).wait_send()
                taps_copy(step).wait_send()

        @pl.when(is_source & (place.along != 0))
        def _():
            for micro in range(micro_count):
                crop_copy(micro).wait_send()

        @pl.when(is_source & (place.along != 3))
        def _():
            label_copy.wait_send()

    def finish(micro, carry):
        @pl.when(jnp.logical_not(is_last))
        def _():
            tile_copy(micro).wait_send()

        @pl.when(jnp.logical_not(is_first))
        def _():
            up_copy(micro).wait_send()

        return carry

    lax.fori_loop(0, micro_count, finish, 0)


def body(crop_maps, target_maps, crop_counts, depth_kernels, weight_in, weight_out, head_weight):
    section_count = lax.axis_size("section")
    micro_count, slots = crop_maps.shape[1:3]
    width = crop_maps.shape[-1]
    cells = slots * SIDE * SIDE
    expand = weight_in.shape[2]
    live = jnp.arange(slots)[None, :] < crop_counts[0][:, None]
    entering = crop_maps[0] * live[:, :, None, None, None].astype(jnp.bfloat16)
    entering = entering.reshape(micro_count, cells, width)
    targets = target_maps[0].reshape(micro_count, cells, 1).astype(jnp.float32)
    weights = jnp.broadcast_to(
        live[:, :, None].astype(jnp.float32), (micro_count, slots, SIDE * SIDE)
    ).reshape(micro_count, cells, 1)
    lane = jnp.arange(LANES)
    labels = jnp.where(lane == 0, targets, 0.0) + jnp.where(lane == 1, weights, 0.0)
    group_count = lax.axis_size("dp")
    height_in, height_out = weight_in.shape[1], weight_out.shape[1]
    inside = (
        section_count == 4
        and group_count == 8
        and height_in % 16 == 0
        and height_out % 16 == 0
        and 2 * height_out % LANES == 0
    )
    first, second = weight_in[0], weight_out[0]
    if not inside:
        first = lax.all_gather(first, "dp", axis=0, tiled=True)
        second = lax.all_gather(second, "dp", axis=0, tiled=True)
    low, full = jnp.bfloat16, jnp.float32
    every = micro_count * cells
    in_vmem = pl.BlockSpec(memory_space=pltpu.VMEM)
    shapes = [
        ((height_in, expand), full) if inside else ((width, expand), low),
        ((height_out, width), full) if inside else ((expand, width), low),
        ((SMALL_ROWS, width), full),
    ]
    scratch = [
        pltpu.VMEM((micro_count, cells, width), low),
        pltpu.VMEM((micro_count, cells, width), low),
        pltpu.VMEM((micro_count, cells, width), low),
        pltpu.VMEM((micro_count, cells, width), low),
        pltpu.VMEM((cells, width), full),
        pltpu.VMEM((every, width), full),
        pltpu.VMEM((every, width), low),
        pltpu.VMEM((every, LANES), full),
        pltpu.VMEM((every, expand), low),
        pltpu.VMEM((every, expand), full),
        pltpu.VMEM((every, expand), low),
        pltpu.VMEM((HEAD_ROW, SIDE, width), full),
        pltpu.VMEM((SMALL_ROWS - HEAD_ROW, width), full),
        pltpu.SemaphoreType.DMA((micro_count,)),
        pltpu.SemaphoreType.DMA((micro_count,)),
        pltpu.SemaphoreType.DMA((micro_count,)),
        pltpu.SemaphoreType.DMA((micro_count,)),
        pltpu.SemaphoreType.DMA((section_count - 1,)),
        pltpu.SemaphoreType.DMA,
    ]
    if inside:
        dma = pltpu.SemaphoreType.DMA
        whole = [pltpu.VMEM((width, expand), low), pltpu.VMEM((expand, width), low)]
        slabs = [
            pltpu.VMEM((4, height_in, expand), low), pltpu.VMEM((4, height_out, width), low)
        ]
        scratch += whole * 3 + slabs * 2
        scratch += [
            pltpu.VMEM((height_in, expand), low),
            pltpu.VMEM((height_out, width), low),
            pltpu.VMEM((4, SMALL_ROWS, width), full),
            pltpu.VMEM((3, SMALL_ROWS, width), full),
            pltpu.VMEM((SMALL_ROWS, width), full),
            pltpu.VMEM(depth_kernels.shape[1:], full),
            pltpu.VMEM(labels.shape, full),
            dma((2, 8)), dma((2,)), dma((8,)), dma((4,)), dma((8,)),
            dma((4,)), dma((4,)), dma((4,)), dma((4,)), dma((4,)), dma((4,)), dma((4,)), dma((2,)),
            dma((3,)), dma((3,)), dma((3,)), dma, dma((micro_count,)), dma, dma,
            dma((3,)), dma,
        ]
    grad_in, grad_out, small = pl.pallas_call(
        functools.partial(
            kernel, section_count, micro_count, slots, inside
        ),
        out_shape=tuple(jax.ShapeDtypeStruct(shape, kind) for shape, kind in shapes),
        in_specs=[in_vmem] * 6,
        out_specs=(in_vmem,) * 3,
        scratch_shapes=scratch,
        compiler_params=pltpu.CompilerParams(
            collective_id=0, has_side_effects=True, vmem_limit_bytes=60 * 1024 * 1024
        ),
        cost_estimate=pl.CostEstimate(
            flops=12 * every * width * expand, bytes_accessed=8 * width * expand, transcendentals=0
        ),
    )(entering, labels, depth_kernels[0], first, second, head_weight[None])
    if not inside:
        grad_in = lax.psum_scatter(grad_in, "dp", scatter_dimension=0, tiled=True).astype(full)
        grad_out = lax.psum_scatter(grad_out, "dp", scatter_dimension=0, tiled=True).astype(full)
        small = lax.psum(small, "dp")
    taps = depth_kernels.shape[1]
    return (
        grad_in[None],
        grad_out[None],
        small[:taps][None],
        small[HEAD_ROW],
        small[HEAD_ROW + 1, 0],
    )


def solution(mesh):
    return jax.shard_map(
        body,
        mesh=mesh,
        in_specs=(
            P("dp", None, None, None, None, None),
            P("dp", None, None, None, None),
            P("dp", None),
            P("section", None, None),
            P("section", "dp", None),
            P("section", "dp", None),
            P(),
        ),
        out_specs=(
            P("section", "dp", None),
            P("section", "dp", None),
            P("section", None, None),
            P(),
            P(),
        ),
        check_vma=False,
    )
```
